128 devices in a mesh: ga: 4 (over y), dev: 32 (over x, z, core).
Axes of the slice: x: 4, y: 4, z: 4, core: 2. Of those that a mesh axis runs over, the one named last changes fastest.
Arguments:
- hidden_in: bfloat16 [1024, 2, 2048], P('dev'), may hold values from -6 to 6
- w_qkv: bfloat16 [2048, 4, 1280], P(None, 'ga'), may hold values from -0.125 to 0.125
- w_out: bfloat16 [4, 1024, 2048], P('ga'), may hold values from -0.09375 to 0.09375
- cache: bfloat16 [1024, 4, 2, 768, 128], P('dev', 'ga'), may hold values from -64 to 64, as said below
- lengths: int32 [1024], P('dev'), may hold values from 96 to 768, as said below
- w_router: bfloat16 [2048, 128], replicated, may hold values from -4 to 4
- routes: int32 [1024, 2, 8], P('dev'), may hold values from 0 to 127, all different within a row; in each aligned block of 64 rows (0 to 63, 64 to 127, ..., all dimensions but the last counted through in order) at most 10 rows name the same one
- w_gate_up: bfloat16 [128, 2048, 1536], P(('ga', 'dev')), may hold values from -0.125 to 0.125
- w_down: bfloat16 [128, 768, 2048], P(('ga', 'dev')), may hold values from -0.21875 to 0.21875
Outputs:
- layer_out: bfloat16 [1024, 2, 2048], P('dev', None, 'ga')
The draws below stay inside these ranges and needn't reach their ends.
Inputs may be any that keep to these rules, and one draw needn't show every extreme that they name: Request r's cache holds lengths[r] live positions, 0 to lengths[r] - 1; its two new tokens stand at positions lengths[r] and lengths[r] + 1. Some request has exactly 768 and some exactly 96. `routes`: A row names 8 different experts. In each aligned block of 64 rows (the tokens of one index of dev, rows counted over requests and draft positions in order) no expert is named by more than 10 rows, a bound that some block reaches. `cache`: positions at or beyond a request's length hold data that is not part of its context.
All inputs are finite; a program needn't handle non-finite values.
Results may differ from the reference program's by a relative error of at most 0.01.
The reference program's roundings to bfloat16 on the way count: a program that leaves them out, or rounds other values in their place, can miss the bound.
Values may be sent and summed in bfloat16 or wider, within the bound.
A program may use at most 128 MiB of HBM per device.

```python
import math
import jax
import jax.numpy as jnp
import numpy as np
from jax import lax

D = 2048
HEADS = 32
KEY_VALUE_HEADS = 4
HD = 128
FF = 768
TOP = 8
DRAFT = 2
R_DEV = 32
CONTEXT_SLOTS = 768
GROUP = 8
EXPERTS = 128
REQUEST_TOTAL = 1024
CAP = 10
N_DEV = 32


def draw_cache(key, part):
    key = jax.random.fold_in(key, 11)
    root_random_key = jax.random.fold_in(key, 0)
    shape = (REQUEST_TOTAL, KEY_VALUE_HEADS, 2, CONTEXT_SLOTS, HD)
    base = jax.random.normal(root_random_key, shape, jnp.float32)
    which = jnp.arange(2, dtype=jnp.float32).reshape(1, 1, 2, 1, 1)
    key_scale = 2.0
    factor = key_scale * (1.0 - which) + which
    return jnp.clip(base * factor, -64.0, 64.0).astype(jnp.bfloat16)


def draw_lengths(key, part):
    key = jax.random.fold_in(key, 37)
    key_one, key_two, key_three, key_four = jax.random.split(key, 4)
    lowest = CONTEXT_SLOTS // 8
    draw_one = jax.random.randint(key_one, (REQUEST_TOTAL,), lowest, CONTEXT_SLOTS + 1)
    draw_two = jax.random.randint(key_two, (REQUEST_TOTAL,), lowest, CONTEXT_SLOTS + 1)
    drawn = jnp.minimum(draw_one, draw_two)
    longest = jax.random.randint(key_three, (), 0, REQUEST_TOTAL)
    offset_pick = jax.random.randint(key_four, (), 1, REQUEST_TOTAL)
    shortest = (longest + offset_pick) % REQUEST_TOTAL
    drawn = drawn.at[longest].set(CONTEXT_SLOTS).at[shortest].set(lowest)
    return drawn.astype(jnp.int32)


def draw_w_router(key, part):
    key = jax.random.fold_in(key, 23)
    root_random_key, column_key = jax.random.split(key)
    base = jax.random.normal(root_random_key, (D, EXPERTS), jnp.float32)
    column = jnp.exp(jax.random.uniform(column_key, (1, EXPERTS), jnp.float32, math.log(0.5), math.log(5.0)))
    return jnp.clip(base * column / math.sqrt(D), -4.0, 4.0).astype(jnp.bfloat16)


def steps_of(rng, extent, cuts, smallest, largest):
    def one(position, parts):
        heights = jax.random.uniform(jax.random.fold_in(jax.random.fold_in(rng, 6), position), (parts,), jnp.float32, smallest / len(cuts), largest / len(cuts))
        return jnp.repeat(jnp.exp(heights), extent[position] // parts).reshape((-1,) + (1,) * (len(extent) - position - 1))

    loudness = one(*cuts[0])
    for cut in cuts[1:]:
        loudness = loudness * one(*cut)
    return loudness


def assign_block(own_key, own, number, rows, count, top, reach, slope):
    ranking = jax.random.permutation(own_key, count)
    crowded, usual = load_shares(count, rows * top, reach, slope, True), load_shares(count, rows * top, reach, slope, False)
    places = jnp.arange(count)

    def named(tallies, rotation):
        used = int((tallies > 0).sum())
        fixed = max(1, used // 4)
        passed = fixed + (places - fixed + rotation * (used - fixed)) % max(1, count - fixed)
        return jnp.zeros((count,), jnp.int32).at[ranking[jnp.where(places < fixed, places, passed)]].set(jnp.asarray(tallies, jnp.int32))

    tallies = jnp.where(number % 4 == 0, named(crowded, number // 4), named(usual, number - number // 4 - 1))
    mixed = jax.random.permutation(jax.random.fold_in(own, 3), count)
    donor, receiver = mixed[0:count // 2 * 2:2], mixed[1:count // 2 * 2:2]
    margin = jnp.minimum(tallies[donor] - 1, reach - tallies[receiver]) // 2
    margin = jnp.where((donor == ranking[0]) | (receiver == ranking[0]) | (tallies[receiver] == 0), 0, jnp.maximum(margin, 0))
    passed = jax.random.randint(jax.random.fold_in(own, 4), (count // 2,), 0, 1 << 20) % (margin + 1)
    tallies = tallies.at[donor].add(-passed).at[receiver].add(passed)
    labels = jnp.searchsorted(jnp.cumsum(tallies), jnp.arange(rows * top), side="right").astype(jnp.int32)
    grid = labels.reshape(top, rows).T
    grid = grid[jax.random.permutation(jax.random.fold_in(own, 1), rows)]
    rotation = jax.random.randint(jax.random.fold_in(own, 2), (rows, 1), 0, top)
    return jnp.take_along_axis(grid, (jnp.arange(top)[None, :] + rotation) % top, axis=1)


def load_shares(count, total, most, slope, full):
    loads = [(1 << 20) // math.isqrt(rank ** slope) + 1 for rank in range(1, count + 1)]
    largest = most if full else min(most, max(-(-total // count), total * loads[0] // sum(loads)))
    least = 1 if total - largest >= count - 1 else 0
    holding, surplus = [largest] + [least] * (count - 1), total - largest - least * (count - 1)
    while surplus > 0:
        movable = [i for i in range(1, count) if holding[i] < largest] or [i for i in range(1, count) if holding[i] < most]
        whole, budget = sum([loads[i] for i in movable]), surplus
        for i in movable:
            more = min(most - holding[i], max(1, budget * loads[i] // whole), surplus)
            holding[i] = holding[i] + more
            surplus = surplus - more
    return np.array(holding)


def gaussian(rng, extent, scale, bound, cuts=(), kind=jnp.bfloat16):
    entries = jax.random.normal(rng, extent, jnp.float32) * scale
    if len(cuts) > 0:
        entries = steps_of(rng, extent, cuts, -0.22, 0.18) * entries
    return jnp.clip(entries, min=-bound, max=bound).astype(kind)


def setup_inputs(seed: int = 0) -> dict:
    seeds = jax.random.split(jax.random.key(seed), 10)
    hidden_in = gaussian(seeds[0], (REQUEST_TOTAL, DRAFT, D), 1.0, 6.0, ((0, 32),))
    w_qkv = gaussian(seeds[1], (D, KEY_VALUE_HEADS, (GROUP + 2) * HD), D ** -0.5, 0.125, ((1, 4),))
    w_out = gaussian(seeds[2], (KEY_VALUE_HEADS, GROUP * HD, D), (HEADS * HD) ** -0.5, 0.09375, ((0, 4),))
    cache = draw_cache(jax.random.fold_in(seeds[9], 71), 0)
    lengths = draw_lengths(jax.random.fold_in(seeds[9], 71), 0)
    w_router = draw_w_router(jax.random.fold_in(seeds[9], 71), 0)
    routes_keys = jax.random.split(jax.random.fold_in(seeds[6], 1), REQUEST_TOTAL * DRAFT // (DRAFT * R_DEV))
    routes_turns = jax.random.permutation(jax.random.fold_in(seeds[6], 3), REQUEST_TOTAL * DRAFT // (DRAFT * R_DEV))
    routes = jax.vmap(lambda own, number: assign_block(jax.random.fold_in(seeds[6], 2), own, number, DRAFT * R_DEV, EXPERTS, TOP, CAP, 2))(routes_keys, routes_turns).reshape((REQUEST_TOTAL, DRAFT, TOP))
    w_gate_up = gaussian(seeds[7], (EXPERTS, D, 2 * FF), D ** -0.5, 0.125, ((0, 128),))
    w_down = gaussian(seeds[8], (EXPERTS, FF, D), FF ** -0.5, 0.21875, ((0, 128),))
    return dict(hidden_in=hidden_in, w_qkv=w_qkv, w_out=w_out, cache=cache, lengths=lengths, w_router=w_router, routes=routes, w_gate_up=w_gate_up, w_down=w_down)


ROPE_BASE = 1000000.0
NORM_EPS = 1e-06

def rotate_half(values, positions):
    half_width = values.shape[-1] // 2
    exponent = jnp.arange(half_width, dtype=jnp.float32) * (2.0 / values.shape[-1])
    angles = positions * ROPE_BASE ** (-exponent)
    cosine = jnp.cos(angles)
    sine_part = jnp.sin(angles)
    first_half = values[..., :half_width]
    second_half = values[..., half_width:]
    return jnp.concatenate([first_half * cosine - second_half * sine_part, second_half * cosine + first_half * sine_part], axis=-1)

def norm_rows(values):
    return values * lax.rsqrt(lax.optimization_barrier(jnp.mean(values * values, axis=-1, keepdims=True)) + NORM_EPS)

def attend_one(packed):
    queries, new_keys, new_values, cache_one, length_one = packed
    draft_len, kv_heads, group_size, head_dim = queries.shape
    score_scale = head_dim ** (-0.5)
    query_f32 = queries.astype(jnp.float32)
    old_scores = jnp.einsum('tkgh,kch->kgtc', query_f32, cache_one[:, 0].astype(jnp.float32)) * score_scale
    fresh_scores = jnp.einsum('tkgh,skh->kgts', query_f32, new_keys.astype(jnp.float32)) * score_scale
    context = cache_one.shape[2]
    old_live = jnp.arange(context, dtype=jnp.int32) < length_one
    fresh_live = jnp.arange(draft_len, dtype=jnp.int32)[None, :] <= jnp.arange(draft_len, dtype=jnp.int32)[:, None]
    old_scores = jnp.where(old_live, old_scores, -jnp.inf)
    fresh_scores = jnp.where(fresh_live, fresh_scores, -jnp.inf)
    row_top = jnp.maximum(lax.optimization_barrier(jnp.max(old_scores, axis=-1)), lax.optimization_barrier(jnp.max(fresh_scores, axis=-1)))[..., None]
    old_exp = jnp.exp(old_scores - row_top)
    fresh_exp = jnp.exp(fresh_scores - row_top)
    totals = lax.optimization_barrier(jnp.sum(old_exp, axis=-1)) + lax.optimization_barrier(jnp.sum(fresh_exp, axis=-1))
    old_weights = lax.optimization_barrier(old_exp.astype(jnp.bfloat16)).astype(jnp.float32)
    fresh_weights = lax.optimization_barrier(fresh_exp.astype(jnp.bfloat16)).astype(jnp.float32)
    mixed_sum = jnp.einsum('kgtc,kch->tkgh', old_weights, cache_one[:, 1].astype(jnp.float32))
    mixed_sum = mixed_sum + jnp.einsum('kgts,skh->tkgh', fresh_weights, new_values.astype(jnp.float32))
    head_out = (mixed_sum / jnp.transpose(totals, (2, 0, 1))[..., None]).astype(jnp.bfloat16)
    return head_out.reshape(draft_len, kv_heads, group_size * head_dim)

def reference(hidden_in, w_qkv, w_out, cache, lengths, w_router, routes, w_gate_up, w_down):
    req_total, draft_len, model_width = hidden_in.shape
    head_dim = cache.shape[-1]
    kv_heads = w_qkv.shape[1]
    group_size = w_qkv.shape[2] // head_dim - 2
    token_f32 = hidden_in.astype(jnp.float32)
    normed = norm_rows(token_f32).astype(jnp.bfloat16)
    projected = jnp.einsum('rtd,dkc->rtkc', normed.astype(jnp.float32), w_qkv.astype(jnp.float32))
    positions = (lengths[:, None] + jnp.arange(draft_len, dtype=jnp.int32)[None, :]).astype(jnp.float32)
    query_part = projected[..., :group_size * head_dim].reshape(req_total, draft_len, kv_heads, group_size, head_dim)
    queries = rotate_half(query_part, positions[:, :, None, None, None]).astype(jnp.bfloat16)
    key_part = projected[..., group_size * head_dim:(group_size + 1) * head_dim]
    new_keys = rotate_half(key_part, positions[:, :, None, None]).astype(jnp.bfloat16)
    new_values = projected[..., (group_size + 1) * head_dim:].astype(jnp.bfloat16)
    head_out = lax.map(attend_one, (queries, new_keys, new_values, cache, lengths))
    attn = jnp.einsum('rtkf,kfd->rtd', head_out.astype(jnp.float32), w_out.astype(jnp.float32))
    residual = (token_f32 + attn).astype(jnp.bfloat16)
    resid_f32 = residual.astype(jnp.float32)
    normed_mid = norm_rows(resid_f32).astype(jnp.bfloat16)
    flat_mid = normed_mid.reshape(-1, model_width)
    flat_routes = routes.reshape(-1, routes.shape[-1])
    logits = jnp.dot(flat_mid, w_router, preferred_element_type=jnp.float32)
    chosen = jnp.take_along_axis(logits, flat_routes, axis=1)
    gates = jax.nn.softmax(chosen, axis=-1)
    expert_count = w_router.shape[1]
    limit_rows = N_DEV * CAP

    def per_expert(total_sum, packed):
        expert_id, gate_up, down_proj = packed
        matches = flat_routes == expert_id
        member = jnp.any(matches, axis=1)
        gate_col = lax.optimization_barrier(jnp.sum(jnp.where(matches, gates, 0.0), axis=1))
        order = jnp.argsort(jnp.where(member, 0, 1).astype(jnp.int32), stable=True)[:limit_rows]
        chosen_rows = flat_mid[order]
        ff_width = down_proj.shape[0]
        mixed_up = jnp.dot(chosen_rows, gate_up, preferred_element_type=jnp.float32)
        activated = (jax.nn.silu(mixed_up[:, :ff_width]) * mixed_up[:, ff_width:]).astype(jnp.bfloat16)
        produced = jnp.dot(activated, down_proj, preferred_element_type=jnp.float32).astype(jnp.bfloat16).astype(jnp.float32)
        total_sum = total_sum.at[order].add(gate_col[order][:, None] * produced)
        return (total_sum, None)
    start_sum = jnp.zeros(flat_mid.shape, jnp.float32)
    moe_sum, unused = lax.scan(per_expert, start_sum, (jnp.arange(expert_count, dtype=jnp.int32), w_gate_up, w_down))
    return (resid_f32 + moe_sum.reshape(resid_f32.shape)).astype(jnp.bfloat16)
```

```python
import jax
import jax.numpy as jnp
from jax import lax
from jax.experimental import pallas as pl
from jax.experimental.pallas import tpu as pltpu
from jax.sharding import PartitionSpec as P

ROPE_BASE = 1000000.0
NORM_EPS = 1e-06


def rotate_half(values, positions):
    half_width = values.shape[-1] // 2
    exponent = jnp.arange(half_width, dtype=jnp.float32) * (2.0 / values.shape[-1])
    angles = positions * ROPE_BASE ** (-exponent)
    cosine = jnp.cos(angles)
    sine_part = jnp.sin(angles)
    first_half = values[..., :half_width]
    second_half = values[..., half_width:]
    return jnp.concatenate(
        [
            first_half * cosine - second_half * sine_part,
            second_half * cosine + first_half * sine_part,
        ],
        axis=-1,
    )


def attend(normed, w_qkv, cache_rows, length_rows):
    head_dim = cache_rows.shape[-1]
    group_size = w_qkv.shape[2] // head_dim - 2
    projected = jnp.einsum("rtd,dkc->rtkc", normed, w_qkv, preferred_element_type=jnp.float32)
    req_count, draft_len, kv_local, unused_width = projected.shape
    positions = (length_rows[:, None] + jnp.arange(draft_len, dtype=jnp.int32)[None, :]).astype(
        jnp.float32
    )
    query_part = projected[..., : group_size * head_dim].reshape(
        req_count, draft_len, kv_local, group_size, head_dim
    )
    queries = rotate_half(query_part, positions[:, :, None, None, None]).astype(jnp.bfloat16)
    key_part = projected[..., group_size * head_dim : (group_size + 1) * head_dim]
    new_keys = rotate_half(key_part, positions[:, :, None, None]).astype(jnp.bfloat16)
    new_values = projected[..., (group_size + 1) * head_dim :].astype(jnp.bfloat16)
    score_scale = head_dim ** (-0.5)
    old_scores = (
        jnp.einsum(
            "rtkgh,rkch->rkgtc", queries, cache_rows[:, :, 0], preferred_element_type=jnp.float32
        )
        * score_scale
    )
    fresh_scores = (
        jnp.einsum("rtkgh,rskh->rkgts", queries, new_keys, preferred_element_type=jnp.float32)
        * score_scale
    )
    context = cache_rows.shape[3]
    old_live = jnp.arange(context, dtype=jnp.int32)[None, :] < length_rows[:, None]
    fresh_live = (
        jnp.arange(draft_len, dtype=jnp.int32)[None, :]
        <= jnp.arange(draft_len, dtype=jnp.int32)[:, None]
    )
    old_scores = jnp.where(old_live[:, None, None, None, :], old_scores, -jnp.inf)
    fresh_scores = jnp.where(fresh_live, fresh_scores, -jnp.inf)
    row_top = jnp.maximum(jnp.max(old_scores, axis=-1), jnp.max(fresh_scores, axis=-1))[..., None]
    old_exp = jnp.exp(old_scores - row_top)
    fresh_exp = jnp.exp(fresh_scores - row_top)
    totals = jnp.sum(old_exp, axis=-1) + jnp.sum(fresh_exp, axis=-1)
    mixed_sum = jnp.einsum(
        "rkgtc,rkch->rtkgh",
        old_exp.astype(jnp.bfloat16),
        cache_rows[:, :, 1],
        preferred_element_type=jnp.float32,
    )
    mixed_sum = mixed_sum + jnp.einsum(
        "rkgts,rskh->rtkgh",
        fresh_exp.astype(jnp.bfloat16),
        new_values,
        preferred_element_type=jnp.float32,
    )
    head_out = (mixed_sum / jnp.transpose(totals, (0, 3, 1, 2))[..., None]).astype(jnp.bfloat16)
    return head_out.reshape(req_count, draft_len, kv_local, group_size * head_dim)


N_GROUPS = 4
N_MEMBERS = 32
TOKENS = 64
WIDTH = 2048
QUARTER = 512
FF = 768
EXPERTS = 128
ROWS = 16 * N_MEMBERS
PACKED = 1280
F32 = jnp.float32
BF16 = jnp.bfloat16


def iota(shape, axis):
    return lax.broadcasted_iota(jnp.int32, shape, axis)


def dot(a, b):
    return jnp.dot(a, b, preferred_element_type=F32)


def dot_nt(a, b):
    return lax.dot_general(a, b, (((1,), (1,)), ((), ())), preferred_element_type=F32)


def one_hot(mask):
    return jnp.where(mask, 1.0, 0.0).astype(BF16)


def layer_kernel(
    heads_ref,
    hidden_ref,
    router_ref,
    routes_ref,
    w_out_hbm,
    gate_up_hbm,
    down_hbm,
    out_ref,
    w_out,
    gate_up,
    down,
    part_out,
    part_in,
    resid,
    mid,
    sel_a,
    sel_b,
    comb_a,
    comb_b,
    send,
    recv,
    back,
    home,
    rows,
    acts,
    made,
    moe_out,
    moe_in,
    load_sem,
    rs_sem,
    ag_sem,
    go_send,
    go_recv,
    back_send,
    back_recv,
    fin_sem,
):
    group = lax.axis_index("ga")
    member = lax.axis_index("dev")

    def peer(offset):
        return lax.rem(group + offset, N_GROUPS)

    def other(offset):
        return lax.rem(member + offset, N_MEMBERS)

    order = (2, 1, 3, 0)
    loads = {}
    for offset in order:
        columns = pl.ds(pl.multiple_of(peer(offset) * QUARTER, QUARTER), QUARTER)
        loads[offset] = pltpu.make_async_copy(
            w_out_hbm.at[:, columns], w_out.at[offset], load_sem.at[offset]
        )
        loads[offset].start()
    load_gate_up = pltpu.make_async_copy(gate_up_hbm, gate_up, load_sem.at[4])
    load_gate_up.start()
    load_down = pltpu.make_async_copy(down_hbm, down, load_sem.at[5])
    load_down.start()

    barrier = pltpu.get_barrier_semaphore()
    for offset in range(1, N_GROUPS):
        pl.semaphore_signal(
            barrier,
            inc=1,
            device_id={"ga": peer(offset)},
            device_id_type=pl.DeviceIdType.MESH,
        )

    @pl.loop(1, N_MEMBERS)
    def _(offset):
        pl.semaphore_signal(
            barrier,
            inc=1,
            device_id={"dev": other(offset)},
            device_id_type=pl.DeviceIdType.MESH,
        )

    heads = heads_ref[...]
    parts = {}
    for place, offset in enumerate(order):
        loads[offset].wait()
        part_out[offset] = dot(heads, w_out[offset])
        if place == 0:
            pl.semaphore_wait(barrier, N_GROUPS - 1 + N_MEMBERS - 1)
        if offset:
            parts[offset] = pltpu.make_async_remote_copy(
                src_ref=part_out.at[offset],
                dst_ref=part_in.at[offset],
                send_sem=rs_sem.at[0, offset],
                recv_sem=rs_sem.at[1, offset],
                device_id={"ga": peer(offset)},
                device_id_type=pl.DeviceIdType.MESH,
            )
            parts[offset].start()

    expert_of = iota((TOKENS, EXPERTS), 1)
    routes = routes_ref[...]
    hit = routes[:, 0:1] == expert_of
    for choice in range(1, routes.shape[1]):
        hit = hit | (routes[:, choice : choice + 1] == expert_of)
    earlier = one_hot(iota((TOKENS, TOKENS), 0) > iota((TOKENS, TOKENS), 1))
    slots = dot(earlier, one_hot(hit))
    code = jnp.where(hit, slots, -1.0).astype(BF16)
    code_a = jnp.concatenate([code] * 2, axis=0)
    code_b = jnp.concatenate([code] * 8, axis=0)
    first = group * N_MEMBERS
    spread = one_hot(iota((ROWS, EXPERTS), 0) // 16 + first == iota((ROWS, EXPERTS), 1))
    gather = one_hot(iota((EXPERTS, ROWS), 1) // 16 + first == iota((EXPERTS, ROWS), 0))

    row, col = iota((ROWS, 2 * TOKENS), 0), iota((ROWS, 2 * TOKENS), 1)
    sel_a[...] = one_hot(
        (dot_nt(spread, code_a) == (row % 8).astype(F32)) & ((row // 8) % 2 == col // TOKENS)
    )
    row, col = iota((ROWS, 8 * TOKENS), 0), iota((ROWS, 8 * TOKENS), 1)
    sel_b[...] = one_hot(
        (dot_nt(spread, code_b) == (8 + row % 2).astype(F32)) & ((row // 2) % 8 == col // TOKENS)
    )
    row, col = iota((2 * TOKENS, ROWS), 0), iota((2 * TOKENS, ROWS), 1)
    mask_a = (dot(code_a, gather) == (col % 8).astype(F32)) & ((col // 8) % 2 == row // TOKENS)
    row, col = iota((8 * TOKENS, ROWS), 0), iota((8 * TOKENS, ROWS), 1)
    mask_b = (dot(code_b, gather) == (8 + col % 2).astype(F32)) & ((col // 2) % 8 == row // TOKENS)

    for offset in (1, 3, 2):
        parts[offset].wait()
    attn = part_out[0] + part_in[1] + part_in[2] + part_in[3]
    own = pl.ds(pl.multiple_of(group * QUARTER, QUARTER), QUARTER)
    resid[group] = (hidden_ref[:, own].astype(F32) + attn).astype(BF16)
    quarters = {}
    for offset in (2, 1, 3):
        quarters[offset] = pltpu.make_async_remote_copy(
            src_ref=resid.at[group],
            dst_ref=resid.at[group],
            send_sem=ag_sem.at[0, offset],
            recv_sem=ag_sem.at[1, offset],
            device_id={"ga": peer(offset)},
            device_id_type=pl.DeviceIdType.MESH,
        )
        quarters[offset].start()
    for offset in (1, 3, 2):
        quarters[offset].wait_send()
        pltpu.make_async_remote_copy(
            src_ref=resid.at[group],
            dst_ref=resid.at[peer(N_GROUPS - offset)],
            send_sem=ag_sem.at[0, offset],
            recv_sem=ag_sem.at[1, offset],
            device_id={"ga": peer(offset)},
            device_id_type=pl.DeviceIdType.MESH,
        ).wait_recv()

    squares = jnp.zeros((TOKENS, 1), F32)
    for quarter in range(N_GROUPS):
        values = resid[quarter].astype(F32)
        squares = squares + jnp.sum(values * values, axis=-1, keepdims=True)
    scale = lax.rsqrt(squares / WIDTH + NORM_EPS)
    for quarter in range(N_GROUPS):
        mid[:, quarter * QUARTER : (quarter + 1) * QUARTER] = (
            resid[quarter].astype(F32) * scale
        ).astype(BF16)

    stacked = jnp.concatenate([mid[:, :1024], mid[:, 1024:]], axis=0)
    packed_a = dot(sel_a[...], stacked).astype(BF16)
    send[:, :, :1024] = packed_a.reshape(N_MEMBERS, 16, 1024)
    stacked = jnp.concatenate([mid[:, 256 * k : 256 * k + 256] for k in range(8)], axis=0)
    packed_b = dot(sel_b[...], stacked).astype(BF16)
    send[:, :, 1024:] = packed_b.reshape(N_MEMBERS, 16, 256)

    def going(offset):
        return pltpu.make_async_remote_copy(
            src_ref=send.at[other(offset)],
            dst_ref=recv.at[member],
            send_sem=go_send.at[offset],
            recv_sem=go_recv.at[offset],
            device_id={"dev": other(offset)},
            device_id_type=pl.DeviceIdType.MESH,
        )

    @pl.loop(1, N_MEMBERS)
    def _(offset):
        going(offset).start()

    recv[member] = send[member]

    logits = dot(mid[...], router_ref[...])
    top = jnp.max(jnp.where(hit, logits, -jnp.inf), axis=-1, keepdims=True)
    raised = jnp.where(hit, jnp.exp(logits - top), 0.0)
    gates = raised / jnp.sum(raised, axis=-1, keepdims=True)
    rest = gates
    for term in range(3):
        piece = rest.astype(BF16)
        rest = rest - piece.astype(F32)
        spread_a = dot(jnp.concatenate([piece] * 2, axis=0), gather)
        comb = jnp.where(mask_a, spread_a, 0.0).astype(BF16)
        for half in range(2):
            comb_a[half, term * TOKENS : (term + 1) * TOKENS] = comb[
                half * TOKENS : (half + 1) * TOKENS
            ]
        spread_b = dot(jnp.concatenate([piece] * 8, axis=0), gather)
        comb = jnp.where(mask_b, spread_b, 0.0).astype(BF16)
        for eighth in range(8):
            comb_b[eighth, term * TOKENS : (term + 1) * TOKENS] = comb[
                eighth * TOKENS : (eighth + 1) * TOKENS
            ]

    load_gate_up.wait()
    load_down.wait()

    @pl.loop(1, N_MEMBERS)
    def _(offset):
        going(offset).wait_send()
        pltpu.make_async_remote_copy(
            src_ref=send.at[other(offset)],
            dst_ref=recv.at[other(N_MEMBERS - offset)],
            send_sem=go_send.at[offset],
            recv_sem=go_recv.at[offset],
            device_id={"dev": other(offset)},
            device_id_type=pl.DeviceIdType.MESH,
        ).wait_recv()

    row, col = iota((ROWS, ROWS), 0), iota((ROWS, ROWS), 1)
    unpack = one_hot(((row % 64) // 2) * 16 + (row // 64) * 2 + row % 2 == col)
    pack = one_hot(((col % 64) // 2) * 16 + (col // 64) * 2 + col % 2 == row)
    got = recv[:, :, :1024].astype(F32)
    for half in range(2):
        rows[:256, half * 1024 : (half + 1) * 1024] = (
            got[:, half * 8 : half * 8 + 8].reshape(256, 1024).astype(BF16)
        )
    sorted_b = dot(unpack, recv[:, :, 1024:].reshape(ROWS, 256)).astype(BF16)
    for k in range(8):
        rows[256:, 256 * k : 256 * k + 256] = sorted_b[64 * k : 64 * k + 64]
    for chunk in range(3):
        columns = slice(256 * chunk, 256 * chunk + 256)
        gate = dot(rows[...], gate_up[:, columns])
        up = dot(rows[...], gate_up[:, FF + 256 * chunk : FF + 256 * chunk + 256])
        acts[:, columns] = (gate / (1.0 + jnp.exp(-gate)) * up).astype(BF16)
    for chunk in range(8):
        result = dot(acts[...], down[:, 256 * chunk : 256 * chunk + 256])
        half, place = chunk // 4, (chunk % 4) * 256
        back[:, half * 8 : half * 8 + 8, place : place + 256] = result[:256].reshape(
            N_MEMBERS, 8, 256
        ).astype(BF16)
        made[64 * chunk : 64 * chunk + 64] = result[256:].astype(BF16)
    back[:, :, 1024:] = dot(pack, made[...]).astype(BF16).reshape(N_MEMBERS, 16, 256)

    def returning(offset):
        return pltpu.make_async_remote_copy(
            src_ref=back.at[other(offset)],
            dst_ref=home.at[member],
            send_sem=back_send.at[offset],
            recv_sem=back_recv.at[offset],
            device_id={"dev": other(offset)},
            device_id_type=pl.DeviceIdType.MESH,
        )

    @pl.loop(1, N_MEMBERS)
    def _(offset):
        returning(offset).start()

    home[member] = back[member]

    @pl.loop(1, N_MEMBERS)
    def _(offset):
        returning(offset).wait_send()
        pltpu.make_async_remote_copy(
            src_ref=back.at[other(offset)],
            dst_ref=home.at[other(N_MEMBERS - offset)],
            send_sem=back_send.at[offset],
            recv_sem=back_recv.at[offset],
            device_id={"dev": other(offset)},
            device_id_type=pl.DeviceIdType.MESH,
        ).wait_recv()

    finals = {}
    for offset in order:
        quarter = peer(offset)
        place = pl.ds(pl.multiple_of((quarter % 2) * QUARTER, QUARTER), QUARTER)
        summed = dot(comb_a[quarter // 2], home[:, :, place].reshape(ROWS, QUARTER))
        summed = summed[:TOKENS] + summed[TOKENS : 2 * TOKENS] + summed[2 * TOKENS :]
        moe_out[offset] = summed
        last = home[:, :, 1024:].reshape(ROWS, 256)
        for k in range(2):
            more = dot(comb_b[2 * quarter + k], last)
            more = more[:TOKENS] + more[TOKENS : 2 * TOKENS] + more[2 * TOKENS :]
            moe_out[offset, :, 256 * k : 256 * k + 256] += more
        if offset:
            finals[offset] = pltpu.make_async_remote_copy(
                src_ref=moe_out.at[offset],
                dst_ref=moe_in.at[offset],
                send_sem=fin_sem.at[0, offset],
                recv_sem=fin_sem.at[1, offset],
                device_id={"ga": peer(offset)},
                device_id_type=pl.DeviceIdType.MESH,
            )
            finals[offset].start()
    for offset in (1, 3, 2):
        finals[offset].wait()
    moe = moe_out[0] + moe_in[1] + moe_in[2] + moe_in[3]
    out_ref[...] = (resid[group].astype(F32) + moe).astype(BF16)


def layer(heads, hidden, w_router, routes, w_out, gate_up, down):
    vmem = pl.BlockSpec(memory_space=pltpu.VMEM)
    hbm = pl.BlockSpec(memory_space=pl.ANY)
    dma = pltpu.SemaphoreType.DMA
    packed = pltpu.VMEM((N_MEMBERS, 16, PACKED), BF16)
    parts = pltpu.VMEM((N_GROUPS, TOKENS, QUARTER), F32)
    return pl.pallas_call(
        layer_kernel,
        out_shape=jax.ShapeDtypeStruct((TOKENS, QUARTER), BF16),
        in_specs=[vmem] * 4 + [hbm] * 3,
        out_specs=vmem,
        scratch_shapes=[
            pltpu.VMEM((N_GROUPS, 1024, QUARTER), BF16),
            pltpu.VMEM((WIDTH, 2 * FF), BF16),
            pltpu.VMEM((FF, WIDTH), BF16),
            parts,
            parts,
            pltpu.VMEM((N_GROUPS, TOKENS, QUARTER), BF16),
            pltpu.VMEM((TOKENS, WIDTH), BF16),
            pltpu.VMEM((ROWS, 2 * TOKENS), BF16),
            pltpu.VMEM((ROWS, 8 * TOKENS), BF16),
            pltpu.VMEM((2, 3 * TOKENS, ROWS), BF16),
            pltpu.VMEM((8, 3 * TOKENS, ROWS), BF16),
            packed,
            packed,
            packed,
            packed,
            pltpu.VMEM((320, WIDTH), BF16),
            pltpu.VMEM((320, FF), BF16),
            pltpu.VMEM((ROWS, 256), BF16),
            parts,
            parts,
            dma((6,)),
            dma((2, N_GROUPS)),
            dma((2, N_GROUPS)),
            dma((N_MEMBERS,)),
            dma((N_MEMBERS,)),
            dma((N_MEMBERS,)),
            dma((N_MEMBERS,)),
            dma((2, N_GROUPS)),
        ],
        compiler_params=pltpu.CompilerParams(
            collective_id=0, has_side_effects=True, vmem_limit_bytes=48 * 1024 * 1024
        ),
    )(heads, hidden, w_router, routes, w_out, gate_up, down)


def body(hidden_in, w_qkv, w_out, cache, lengths, w_router, routes, w_gate_up, w_down):
    req_count, draft_len, model_width = hidden_in.shape
    token_f32 = hidden_in.astype(jnp.float32)
    normed = (
        token_f32 * lax.rsqrt(jnp.mean(token_f32 * token_f32, axis=-1, keepdims=True) + NORM_EPS)
    ).astype(jnp.bfloat16)
    head_out = attend(normed, w_qkv, cache, lengths)
    out = layer(
        head_out.reshape(TOKENS, 1024),
        hidden_in.reshape(TOKENS, model_width),
        w_router,
        routes.reshape(TOKENS, 8),
        w_out[0],
        w_gate_up[0],
        w_down[0],
    )
    return out.reshape(req_count, draft_len, QUARTER)


def solution(mesh):
    return jax.shard_map(
        body,
        mesh=mesh,
        in_specs=(
            P("dev", None, None),
            P(None, "ga", None),
            P("ga", None, None),
            P("dev", "ga", None, None, None),
            P("dev"),
            P(),
            P("dev", None, None),
            P(("ga", "dev"), None, None),
            P(("ga", "dev"), None, None),
        ),
        out_specs=P("dev", None, "ga"),
        check_vma=False,
    )
```

```python
import jax
import jax.numpy as jnp
from jax import lax
from jax.experimental import pallas as pl
from jax.experimental.pallas import tpu as pltpu
from jax.sharding import PartitionSpec as P

ROPE_BASE = 1000000.0
NORM_EPS = 1e-06


N_GROUPS = 4
N_MEMBERS = 32
TOKENS = 64
WIDTH = 2048
QUARTER = 512
FF = 768
EXPERTS = 128
REQUESTS = 32
HD = 128
HEADS = 8
CONTEXT = 768
STEP = 4
ROWS = 16 * N_MEMBERS
PACKED = 1280
FAR_FIRST = sorted(
    range(1, N_MEMBERS),
    key=lambda offset: -min(offset // 8, 4 - offset // 8)
    - min(offset // 2 % 4, 4 - offset // 2 % 4),
)
F32 = jnp.float32
BF16 = jnp.bfloat16


def iota(shape, axis):
    return lax.broadcasted_iota(jnp.int32, shape, axis)


def dot(a, b):
    return jnp.dot(a, b, preferred_element_type=F32)


def dot_nt(a, b):
    return lax.dot_general(a, b, (((1,), (1,)), ((), ())), preferred_element_type=F32)


def one_hot(mask):
    return jnp.where(mask, 1.0, 0.0).astype(BF16)


def layer_kernel(
    lengths_ref,
    speeds_ref,
    hidden_ref,
    router_ref,
    routes_ref,
    w_qkv_hbm,
    cache_hbm,
    w_out_hbm,
    gate_up_hbm,
    down_hbm,
    out_ref,
    w_qkv,
    cache,
    queries,
    fresh,
    head_out,
    w_out,
    gate_up,
    down,
    part_out,
    part_in,
    resid,
    mid,
    sel_a,
    sel_b,
    comb_a,
    comb_b,
    send,
    recv,
    back,
    home,
    rows,
    acts,
    made,
    moe_out,
    moe_in,
    qkv_sem,
    cache_sem,
    load_sem,
    rs_sem,
    ag_sem,
    go_send,
    go_recv,
    back_send,
    back_recv,
    fin_sem,
):
    group = lax.axis_index("ga")
    member = lax.axis_index("dev")

    def peer(offset):
        return lax.rem(group + offset, N_GROUPS)

    x, z, core = member // 8, (member // 2) % 4, member % 2

    def other(offset):
        return (
            ((x + offset // 8) % 4) * 8
            + ((z + (offset // 2) % 4) % 4) * 2
            + (core + offset % 2) % 2
        )

    def source(offset):
        return (
            ((x + 4 - offset // 8) % 4) * 8
            + ((z + 4 - (offset // 2) % 4) % 4) * 2
            + (core + offset % 2) % 2
        )

    qkv_loads = [
        pltpu.make_async_copy(
            w_qkv_hbm.at[:, pl.ds(256 * chunk, 256)], w_qkv.at[chunk], qkv_sem.at[chunk]
        )
        for chunk in range(5)
    ]
    for load in qkv_loads:
        load.start()

    def cache_load(step):
        block = pl.ds(step * STEP, STEP)
        return pltpu.make_async_copy(
            cache_hbm.at[block], cache.at[block], cache_sem.at[step]
        )

    for step in range(REQUESTS // STEP):
        cache_load(step).start()
    order = (2, 1, 3, 0)
    loads = {}
    for offset in order:
        columns = pl.ds(pl.multiple_of(peer(offset) * QUARTER, QUARTER), QUARTER)
        loads[offset] = pltpu.make_async_copy(
            w_out_hbm.at[:, columns], w_out.at[offset], load_sem.at[offset]
        )
        loads[offset].start()
    load_gate_up = pltpu.make_async_copy(gate_up_hbm, gate_up, load_sem.at[4])
    load_gate_up.start()
    load_down = pltpu.make_async_copy(down_hbm, down, load_sem.at[5])
    load_down.start()

    barrier = pltpu.get_barrier_semaphore()
    for offset in range(1, N_GROUPS):
        pl.semaphore_signal(
            barrier,
            inc=1,
            device_id={"ga": peer(offset)},
            device_id_type=pl.DeviceIdType.MESH,
        )

    @pl.loop(1, N_MEMBERS)
    def _(offset):
        pl.semaphore_signal(
            barrier,
            inc=1,
            device_id={"dev": other(offset)},
            device_id_type=pl.DeviceIdType.MESH,
        )

    row = iota((TOKENS, HD), 0)
    places = (row % 2).astype(F32)
    for request in range(REQUESTS):
        length = lengths_ref[request].astype(F32)
        places = places + jnp.where(row // 2 == request, length, 0.0)
    angles = places * speeds_ref[...]
    cosine = jnp.cos(angles)
    sine = jnp.sin(angles)
    sine = jnp.where(iota((TOKENS, HD), 1) < HD // 2, -sine, sine)

    def rotate(values):
        return (values * cosine + pltpu.roll(values, HD // 2, 1) * sine).astype(BF16)

    tokens = hidden_ref[...].astype(F32)
    scale = lax.rsqrt(jnp.mean(tokens * tokens, axis=-1, keepdims=True) + NORM_EPS)
    normed = (tokens * scale).astype(BF16)

    stacked = []
    for chunk in range(4):
        qkv_loads[chunk].wait()
        projected = dot(normed, w_qkv[chunk])
        stacked += [rotate(projected[:, :HD]), rotate(projected[:, HD:])]
    row, col = iota((ROWS, ROWS), 0), iota((ROWS, ROWS), 1)
    by_request = one_hot(((row // 2) % 8) * TOKENS + (row // 16) * 2 + row % 2 == col)
    by_head = one_hot(((col // 2) % 8) * TOKENS + (col // 16) * 2 + col % 2 == row)
    sorted_queries = dot(by_request, jnp.concatenate(stacked, axis=0)).astype(BF16)
    queries[...] = sorted_queries.reshape(REQUESTS, 16, HD)
    qkv_loads[4].wait()
    projected = dot(normed, w_qkv[4])
    new_keys = rotate(projected[:, :HD])
    new_values = projected[:, HD:].astype(BF16)
    row, col = iota((ROWS, TOKENS), 0), iota((ROWS, TOKENS), 1)
    visible = (col // 2 == row // 16) & (col % 2 <= row % 2)
    fresh_scores = dot_nt(sorted_queries, new_keys) * HD**-0.5
    fresh[...] = jnp.where(visible, fresh_scores, -jnp.inf).reshape(REQUESTS, 16, TOKENS)

    spot = iota((16, CONTEXT), 1)

    @pl.loop(0, REQUESTS // STEP)
    def _(step):
        cache_load(step).wait()
        for inner in range(STEP):
            request = step * STEP + inner
            scores = dot_nt(queries[request], cache[request, 0]) * HD**-0.5
            scores = jnp.where(spot < lengths_ref[request], scores, -jnp.inf)
            new_scores = fresh[request]
            top = jnp.maximum(
                jnp.max(scores, axis=-1, keepdims=True),
                jnp.max(new_scores, axis=-1, keepdims=True),
            )
            old_exp = jnp.exp(scores - top)
            new_exp = jnp.exp(new_scores - top)
            totals = jnp.sum(old_exp, axis=-1, keepdims=True) + jnp.sum(
                new_exp, axis=-1, keepdims=True
            )
            mixed = dot(old_exp.astype(BF16), cache[request, 1])
            mixed = mixed + dot(new_exp.astype(BF16), new_values)
            head_out[request] = (mixed / totals).astype(BF16)

    by_heads = dot(by_head, head_out[...].reshape(ROWS, HD)).astype(BF16)
    heads = jnp.concatenate(
        [by_heads[TOKENS * head : TOKENS * head + TOKENS] for head in range(HEADS)], axis=1
    )

    parts = {}
    for place, offset in enumerate(order):
        loads[offset].wait()
        part_out[offset] = dot(heads, w_out[offset])
        if place == 0:
            pl.semaphore_wait(barrier, N_GROUPS - 1 + N_MEMBERS - 1)
        if offset:
            parts[offset] = pltpu.make_async_remote_copy(
                src_ref=part_out.at[offset],
                dst_ref=part_in.at[offset],
                send_sem=rs_sem.at[0, offset],
                recv_sem=rs_sem.at[1, offset],
                device_id={"ga": peer(offset)},
                device_id_type=pl.DeviceIdType.MESH,
            )
            parts[offset].start()

    expert_of = iota((TOKENS, EXPERTS), 1)
    routes = routes_ref[...]
    hit = routes[:, 0:1] == expert_of
    for choice in range(1, routes.shape[1]):
        hit = hit | (routes[:, choice : choice + 1] == expert_of)
    earlier = one_hot(iota((TOKENS, TOKENS), 0) > iota((TOKENS, TOKENS), 1))
    slots = dot(earlier, one_hot(hit))
    code = jnp.where(hit, slots, -1.0).astype(BF16)
    code_a = jnp.concatenate([code] * 2, axis=0)
    code_b = jnp.concatenate([code] * 8, axis=0)
    first = group * N_MEMBERS
    spread = one_hot(iota((ROWS, EXPERTS), 0) // 16 + first == iota((ROWS, EXPERTS), 1))
    gather = one_hot(iota((EXPERTS, ROWS), 1) // 16 + first == iota((EXPERTS, ROWS), 0))

    row, col = iota((ROWS, 2 * TOKENS), 0), iota((ROWS, 2 * TOKENS), 1)
    sel_a[...] = one_hot(
        (dot_nt(spread, code_a) == (row % 8).astype(F32)) & ((row // 8) % 2 == col // TOKENS)
    )
    row, col = iota((ROWS, 8 * TOKENS), 0), iota((ROWS, 8 * TOKENS), 1)
    sel_b[...] = one_hot(
        (dot_nt(spread, code_b) == (8 + row % 2).astype(F32)) & ((row // 2) % 8 == col // TOKENS)
    )
    row, col = iota((2 * TOKENS, ROWS), 0), iota((2 * TOKENS, ROWS), 1)
    mask_a = (dot(code_a, gather) == (col % 8).astype(F32)) & ((col // 8) % 2 == row // TOKENS)
    row, col = iota((8 * TOKENS, ROWS), 0), iota((8 * TOKENS, ROWS), 1)
    mask_b = (dot(code_b, gather) == (8 + col % 2).astype(F32)) & ((col // 2) % 8 == row // TOKENS)

    for offset in (1, 3, 2):
        parts[offset].wait()
    attn = part_out[0] + part_in[1] + part_in[2] + part_in[3]
    own = pl.ds(pl.multiple_of(group * QUARTER, QUARTER), QUARTER)
    resid[group] = (hidden_ref[:, own].astype(F32) + attn).astype(BF16)
    quarters = {}
    for offset in (2, 1, 3):
        quarters[offset] = pltpu.make_async_remote_copy(
            src_ref=resid.at[group],
            dst_ref=resid.at[group],
            send_sem=ag_sem.at[0, offset],
            recv_sem=ag_sem.at[1, offset],
            device_id={"ga": peer(offset)},
            device_id_type=pl.DeviceIdType.MESH,
        )
        quarters[offset].start()
    for offset in (1, 3, 2):
        quarters[offset].wait_send()
        pltpu.make_async_remote_copy(
            src_ref=resid.at[group],
            dst_ref=resid.at[peer(N_GROUPS - offset)],
            send_sem=ag_sem.at[0, offset],
            recv_sem=ag_sem.at[1, offset],
            device_id={"ga": peer(offset)},
            device_id_type=pl.DeviceIdType.MESH,
        ).wait_recv()

    squares = jnp.zeros((TOKENS, 1), F32)
    for quarter in range(N_GROUPS):
        values = resid[quarter].astype(F32)
        squares = squares + jnp.sum(values * values, axis=-1, keepdims=True)
    scale = lax.rsqrt(squares / WIDTH + NORM_EPS)
    for quarter in range(N_GROUPS):
        mid[:, quarter * QUARTER : (quarter + 1) * QUARTER] = (
            resid[quarter].astype(F32) * scale
        ).astype(BF16)

    stacked = jnp.concatenate([mid[:, :1024], mid[:, 1024:]], axis=0)
    packed_a = dot(sel_a[...], stacked).astype(BF16)
    send[:, :, :1024] = packed_a.reshape(N_MEMBERS, 16, 1024)
    stacked = jnp.concatenate([mid[:, 256 * k : 256 * k + 256] for k in range(8)], axis=0)
    packed_b = dot(sel_b[...], stacked).astype(BF16)
    send[:, :, 1024:] = packed_b.reshape(N_MEMBERS, 16, 256)

    def going(offset):
        return pltpu.make_async_remote_copy(
            src_ref=send.at[other(offset)],
            dst_ref=recv.at[offset],
            send_sem=go_send.at[offset],
            recv_sem=go_recv.at[offset],
            device_id={"dev": other(offset)},
            device_id_type=pl.DeviceIdType.MESH,
        )

    for offset in FAR_FIRST:
        going(offset).start()
    recv[0] = send[member]

    logits = dot(mid[...], router_ref[...])
    top = jnp.max(jnp.where(hit, logits, -jnp.inf), axis=-1, keepdims=True)
    raised = jnp.where(hit, jnp.exp(logits - top), 0.0)
    gates = raised / jnp.sum(raised, axis=-1, keepdims=True)
    rest = gates
    for term in range(3):
        piece = rest.astype(BF16)
        rest = rest - piece.astype(F32)
        spread_a = dot(jnp.concatenate([piece] * 2, axis=0), gather)
        comb = jnp.where(mask_a, spread_a, 0.0).astype(BF16)
        for half in range(2):
            comb_a[half, term * TOKENS : (term + 1) * TOKENS] = comb[
                half * TOKENS : (half + 1) * TOKENS
            ]
        spread_b = dot(jnp.concatenate([piece] * 8, axis=0), gather)
        comb = jnp.where(mask_b, spread_b, 0.0).astype(BF16)
        for eighth in range(8):
            comb_b[eighth, term * TOKENS : (term + 1) * TOKENS] = comb[
                eighth * TOKENS : (eighth + 1) * TOKENS
            ]

    load_gate_up.wait()
    load_down.wait()

    @pl.loop(1, N_MEMBERS)
    def _(offset):
        going(offset).wait_send()
        pltpu.make_async_remote_copy(
            src_ref=send.at[other(offset)],
            dst_ref=recv.at[offset],
            send_sem=go_send.at[offset],
            recv_sem=go_recv.at[offset],
            device_id={"dev": other(offset)},
            device_id_type=pl.DeviceIdType.MESH,
        ).wait_recv()

    row, col = iota((ROWS, ROWS), 0), iota((ROWS, ROWS), 1)
    unpack = one_hot(((row % 64) // 2) * 16 + (row // 64) * 2 + row % 2 == col)
    pack = one_hot(((col % 64) // 2) * 16 + (col // 64) * 2 + col % 2 == row)
    got = recv[:, :, :1024].astype(F32)
    for half in range(2):
        rows[:256, half * 1024 : (half + 1) * 1024] = (
            got[:, half * 8 : half * 8 + 8].reshape(256, 1024).astype(BF16)
        )
    sorted_b = dot(unpack, recv[:, :, 1024:].reshape(ROWS, 256)).astype(BF16)
    for k in range(8):
        rows[256:, 256 * k : 256 * k + 256] = sorted_b[64 * k : 64 * k + 64]
    for chunk in range(3):
        columns = slice(256 * chunk, 256 * chunk + 256)
        gate = dot(rows[...], gate_up[:, columns])
        up = dot(rows[...], gate_up[:, FF + 256 * chunk : FF + 256 * chunk + 256])
        acts[:, columns] = (gate / (1.0 + jnp.exp(-gate)) * up).astype(BF16)
    for chunk in range(8):
        result = dot(acts[...], down[:, 256 * chunk : 256 * chunk + 256])
        half, place = chunk // 4, (chunk % 4) * 256
        back[:, half * 8 : half * 8 + 8, place : place + 256] = result[:256].reshape(
            N_MEMBERS, 8, 256
        ).astype(BF16)
        made[64 * chunk : 64 * chunk + 64] = result[256:].astype(BF16)
    back[:, :, 1024:] = dot(pack, made[...]).astype(BF16).reshape(N_MEMBERS, 16, 256)

    def returning(offset):
        return pltpu.make_async_remote_copy(
            src_ref=back.at[offset],
            dst_ref=home.at[member],
            send_sem=back_send.at[offset],
            recv_sem=back_recv.at[offset],
            device_id={"dev": source(offset)},
            device_id_type=pl.DeviceIdType.MESH,
        )

    for offset in FAR_FIRST:
        returning(offset).start()
    home[member] = back[0]

    @pl.loop(1, N_MEMBERS)
    def _(offset):
        returning(offset).wait_send()
        pltpu.make_async_remote_copy(
            src_ref=back.at[offset],
            dst_ref=home.at[other(offset)],
            send_sem=back_send.at[offset],
            recv_sem=back_recv.at[offset],
            device_id={"dev": source(offset)},
            device_id_type=pl.DeviceIdType.MESH,
        ).wait_recv()

    finals = {}
    for offset in order:
        quarter = peer(offset)
        place = pl.ds(pl.multiple_of((quarter % 2) * QUARTER, QUARTER), QUARTER)
        summed = dot(comb_a[quarter // 2], home[:, :, place].reshape(ROWS, QUARTER))
        summed = summed[:TOKENS] + summed[TOKENS : 2 * TOKENS] + summed[2 * TOKENS :]
        moe_out[offset] = summed
        last = home[:, :, 1024:].reshape(ROWS, 256)
        for k in range(2):
            more = dot(comb_b[2 * quarter + k], last)
            more = more[:TOKENS] + more[TOKENS : 2 * TOKENS] + more[2 * TOKENS :]
            moe_out[offset, :, 256 * k : 256 * k + 256] += more
        if offset:
            finals[offset] = pltpu.make_async_remote_copy(
                src_ref=moe_out.at[offset],
                dst_ref=moe_in.at[offset],
                send_sem=fin_sem.at[0, offset],
                recv_sem=fin_sem.at[1, offset],
                device_id={"ga": peer(offset)},
                device_id_type=pl.DeviceIdType.MESH,
            )
            finals[offset].start()
    for offset in (1, 3, 2):
        finals[offset].wait()
    moe = moe_out[0] + moe_in[1] + moe_in[2] + moe_in[3]
    out_ref[...] = (resid[group].astype(F32) + moe).astype(BF16)


def layer(lengths, speeds, hidden, w_router, routes, w_qkv, cache, w_out, gate_up, down):
    smem = pl.BlockSpec(memory_space=pltpu.SMEM)
    vmem = pl.BlockSpec(memory_space=pltpu.VMEM)
    hbm = pl.BlockSpec(memory_space=pl.ANY)
    dma = pltpu.SemaphoreType.DMA
    packed = pltpu.VMEM((N_MEMBERS, 16, PACKED), BF16)
    parts = pltpu.VMEM((N_GROUPS, TOKENS, QUARTER), F32)
    return pl.pallas_call(
        layer_kernel,
        out_shape=jax.ShapeDtypeStruct((TOKENS, QUARTER), BF16),
        in_specs=[smem] + [vmem] * 4 + [hbm] * 5,
        out_specs=vmem,
        scratch_shapes=[
            pltpu.VMEM((5, WIDTH, 256), BF16),
            pltpu.VMEM((REQUESTS, 2, CONTEXT, HD), BF16),
            pltpu.VMEM((REQUESTS, 16, HD), BF16),
            pltpu.VMEM((REQUESTS, 16, TOKENS), F32),
            pltpu.VMEM((REQUESTS, 16, HD), BF16),
            pltpu.VMEM((N_GROUPS, 1024, QUARTER), BF16),
            pltpu.VMEM((WIDTH, 2 * FF), BF16),
            pltpu.VMEM((FF, WIDTH), BF16),
            parts,
            parts,
            pltpu.VMEM((N_GROUPS, TOKENS, QUARTER), BF16),
            pltpu.VMEM((TOKENS, WIDTH), BF16),
            pltpu.VMEM((ROWS, 2 * TOKENS), BF16),
            pltpu.VMEM((ROWS, 8 * TOKENS), BF16),
            pltpu.VMEM((2, 3 * TOKENS, ROWS), BF16),
            pltpu.VMEM((8, 3 * TOKENS, ROWS), BF16),
            packed,
            packed,
            packed,
            packed,
            pltpu.VMEM((320, WIDTH), BF16),
            pltpu.VMEM((320, FF), BF16),
            pltpu.VMEM((ROWS, 256), BF16),
            parts,
            parts,
            dma((5,)),
            dma((REQUESTS // STEP,)),
            dma((6,)),
            dma((2, N_GROUPS)),
            dma((2, N_GROUPS)),
            dma((N_MEMBERS,)),
            dma((N_MEMBERS,)),
            dma((N_MEMBERS,)),
            dma((N_MEMBERS,)),
            dma((2, N_GROUPS)),
        ],
        compiler_params=pltpu.CompilerParams(
            collective_id=0, has_side_effects=True, vmem_limit_bytes=56 * 1024 * 1024
        ),
    )(lengths, speeds, hidden, w_router, routes, w_qkv, cache, w_out, gate_up, down)


def body(hidden_in, w_qkv, w_out, cache, lengths, w_router, routes, w_gate_up, w_down):
    req_count, draft_len, model_width = hidden_in.shape
    exponent = jnp.arange(HD // 2, dtype=F32) * (2.0 / HD)
    speeds = ROPE_BASE ** (-exponent)
    out = layer(
        lengths,
        jnp.concatenate([speeds, speeds])[None, :],
        hidden_in.reshape(TOKENS, model_width),
        w_router,
        routes.reshape(TOKENS, 8),
        w_qkv[:, 0],
        cache[:, 0],
        w_out[0],
        w_gate_up[0],
        w_down[0],
    )
    return out.reshape(req_count, draft_len, QUARTER)


def solution(mesh):
    return jax.shard_map(
        body,
        mesh=mesh,
        in_specs=(
            P("dev", None, None),
            P(None, "ga", None),
            P("ga", None, None),
            P("dev", "ga", None, None, None),
            P("dev"),
            P(),
            P("dev", None, None),
            P(("ga", "dev"), None, None),
            P(("ga", "dev"), None, None),
        ),
        out_specs=P("dev", None, "ga"),
        check_vma=False,
    )
```

```python
import jax
import jax.numpy as jnp
import numpy as np
from jax import lax
from jax.experimental import pallas as pl
from jax.experimental.pallas import tpu as pltpu
from jax.sharding import PartitionSpec as P

ROPE_BASE = 1000000.0
NORM_EPS = 1e-06
N_GROUPS = 4
N_MEMBERS = 32
TOKENS = 64
WIDTH = 2048
QUARTER = 512
FF = 768
EXPERTS = 128
REQUESTS = 32
HD = 128
HEADS = 8
CONTEXT = 768
BATCH = 8
ROWS = 16 * N_MEMBERS
PACKED = 640
MESH = pl.DeviceIdType.MESH
F32 = jnp.float32
BF16 = jnp.bfloat16


def iota(shape, axis):
    return lax.broadcasted_iota(jnp.int32, shape, axis)


def dot(a, b):
    return jnp.dot(a, b, preferred_element_type=F32)


def dot_nt(a, b):
    return lax.dot_general(a, b, (((1,), (1,)), ((), ())), preferred_element_type=F32)


def one_hot(mask):
    return jnp.where(mask, 1.0, 0.0).astype(BF16)


def layer_kernel(
    lengths_ref,
    speeds_ref,
    hidden_ref,
    router_ref,
    routes_ref,
    w_qkv_hbm,
    cache_hbm,
    w_out_hbm,
    gate_up_hbm,
    down_hbm,
    out_ref,
    w_qkv,
    cache,
    tokens,
    head_out,
    w_out,
    gate_up,
    down,
    part_out,
    part_in,
    resid,
    mid,
    sel_a,
    sel_b,
    comb_a,
    comb_b,
    send,
    relay,
    recv,
    back,
    back_relay,
    home,
    rows,
    inner_sums,
    acts,
    made,
    moe_out,
    moe_in,
    qkv_sem,
    cache_sem,
    load_sem,
    gate_sem,
    rs_sem,
    ag_sem,
    go_first,
    go_second,
    back_first,
    back_second,
    fin_sem,
):
    group = lax.axis_index("ga")
    member = lax.axis_index("dev")
    x, z, core = member // 8, (member // 2) % 4, member % 2

    def peer(offset):
        return lax.rem(group + offset, N_GROUPS)

    def other(offset):
        return (
            ((x + offset // 8) % 4) * 8
            + ((z + offset % 4) % 4) * 2
            + (core + (offset // 4) % 2) % 2
        )

    def mirror(offset):
        return (
            ((x + 4 - offset // 8) % 4) * 8
            + ((z + 4 - offset % 4) % 4) * 2
            + (core + (offset // 4) % 2) % 2
        )

    qkv_loads = [
        pltpu.make_async_copy(
            w_qkv_hbm.at[:, pl.ds(256 * chunk, 256)], w_qkv.at[chunk], qkv_sem.at[chunk]
        )
        for chunk in range(5)
    ]
    for load in qkv_loads:
        load.start()

    def cache_load(batch):
        block = pl.ds(batch * BATCH, BATCH)
        return pltpu.make_async_copy(
            cache_hbm.at[block], cache.at[block], cache_sem.at[batch]
        )

    cache_load(0).start()
    cache_load(1).start()
    order = (2, 1, 3, 0)
    loads = {}
    for offset in order:
        columns = pl.ds(pl.multiple_of(peer(offset) * QUARTER, QUARTER), QUARTER)
        loads[offset] = pltpu.make_async_copy(
            w_out_hbm.at[:, columns], w_out.at[offset], load_sem.at[offset]
        )
        loads[offset].start()
    cache_load(2).start()
    cache_load(3).start()
    load_gate_up = [
        pltpu.make_async_copy(
            gate_up_hbm.at[pl.ds(QUARTER * quarter + 256 * half, 256)],
            gate_up.at[half, pl.ds(256 * quarter, 256)],
            gate_sem.at[half, quarter],
        )
        for half in range(2)
        for quarter in range(N_GROUPS)
    ]
    for load in load_gate_up:
        load.start()
    load_down = pltpu.make_async_copy(down_hbm, down, load_sem.at[4])
    load_down.start()

    barrier = pltpu.get_barrier_semaphore()
    for offset in range(1, N_GROUPS):
        pl.semaphore_signal(
            barrier, inc=1, device_id={"ga": peer(offset)}, device_id_type=MESH
        )
    for offset in list(range(1, 8)) + [8, 16, 24]:
        pl.semaphore_signal(
            barrier, inc=1, device_id={"dev": other(offset)}, device_id_type=MESH
        )

    row = iota((TOKENS, HD), 0)
    places = (row % 2).astype(F32)
    for request in range(REQUESTS):
        length = lengths_ref[request].astype(F32)
        places = places + jnp.where(row // 2 == request, length, 0.0)
    angles = places * speeds_ref[...]
    cosine = jnp.cos(angles)
    sine = jnp.sin(angles)
    sine = jnp.where(iota((TOKENS, HD), 1) < HD // 2, -sine, sine)

    def rotate(values):
        return (values * cosine + pltpu.roll(values, HD // 2, 1) * sine).astype(BF16)

    hidden = hidden_ref[...].astype(F32).reshape(TOKENS, WIDTH)
    tokens[...] = hidden.astype(BF16)
    scale = lax.rsqrt(jnp.mean(hidden * hidden, axis=-1, keepdims=True) + NORM_EPS)
    normed = (hidden * scale).astype(BF16)

    stacked = []
    for chunk in range(4):
        qkv_loads[chunk].wait()
        projected = dot(normed, w_qkv[chunk])
        stacked += [rotate(projected[:, :HD]), rotate(projected[:, HD:])]
    row, col = iota((ROWS, ROWS), 0), iota((ROWS, ROWS), 1)
    by_request = one_hot(((row // 2) % 8) * TOKENS + (row // 16) * 2 + row % 2 == col)
    row, col = iota((256, 256), 0), iota((256, 256), 1)
    by_head = one_hot(((col // 2) % 8) * 32 + (col // 16) * 2 + col % 2 == row)
    queries = dot(by_request, jnp.concatenate(stacked, axis=0))
    qkv_loads[4].wait()
    projected = dot(normed, w_qkv[4])
    new_keys = rotate(projected[:, :HD])
    new_values = projected[:, HD:].astype(BF16)

    lane = iota((1, HD), 1)
    owner = iota((HD, HD), 1) // 16
    spot = iota((CONTEXT, HD), 0)
    row, col = iota((16, HD), 0), iota((16, HD), 1)
    visible = (row // 2 == col // 16) & (row % 2 <= col % 2)

    def score(batch):
        cache_load(batch).wait()
        first = batch * BATCH
        turned = queries[128 * batch : 128 * batch + 128].T
        blocks = [
            jnp.where(owner == inner, turned, 0.0).astype(BF16) for inner in range(BATCH)
        ]
        scores = dot(
            jnp.concatenate([cache[first + inner, 0] for inner in range(BATCH)], axis=1),
            jnp.concatenate(blocks, axis=0),
        )
        fresh = dot(new_keys[16 * batch : 16 * batch + 16], turned.astype(BF16))
        return scores, fresh

    def mix(batch, scores, fresh):
        first = batch * BATCH
        limits = jnp.zeros((1, HD), jnp.int32)
        for inner in range(BATCH):
            limits = jnp.where(lane // 16 == inner, lengths_ref[first + inner], limits)
        scores = jnp.where(spot < limits, scores * HD**-0.5, -jnp.inf)
        fresh = jnp.where(visible, fresh * HD**-0.5, -jnp.inf)
        top = jnp.maximum(
            jnp.max(scores, axis=0, keepdims=True), jnp.max(fresh, axis=0, keepdims=True)
        )
        old_exp = jnp.exp(scores - top)
        new_exp = jnp.exp(fresh - top)
        totals = jnp.sum(old_exp, axis=0, keepdims=True) + jnp.sum(
            new_exp, axis=0, keepdims=True
        )
        totals = jnp.broadcast_to(totals, (HD, HD)).T
        weights = old_exp.astype(BF16).T
        mixed = [
            dot(weights[16 * inner : 16 * inner + 16], cache[first + inner, 1])
            for inner in range(BATCH)
        ]
        mixed = jnp.concatenate(mixed, axis=0) + dot(
            new_exp.T.astype(BF16), new_values[16 * batch : 16 * batch + 16]
        )
        head_out[128 * batch : 128 * batch + 128] = (mixed / totals).astype(BF16)

    def part_copy(half, offset):
        return pltpu.make_async_remote_copy(
            src_ref=part_out.at[half, offset],
            dst_ref=part_in.at[half, offset],
            send_sem=rs_sem.at[0, half, offset],
            recv_sem=rs_sem.at[1, half, offset],
            device_id={"ga": peer(offset)},
            device_id_type=MESH,
        )

    def project(half):
        by_heads = dot(by_head, head_out[256 * half : 256 * half + 256]).astype(BF16)
        heads = jnp.concatenate(
            [by_heads[32 * head : 32 * head + 32] for head in range(HEADS)], axis=1
        )
        for place, offset in enumerate(order):
            if half == 0:
                loads[offset].wait()
            part_out[half, offset] = dot(heads, w_out[offset])
            if half == 0 and place == 0:
                pl.semaphore_wait(barrier, 13)
            if offset:
                part_copy(half, offset).start()

    def quarter_copy(half, offset, place):
        return pltpu.make_async_remote_copy(
            src_ref=resid.at[half, group],
            dst_ref=resid.at[half, place],
            send_sem=ag_sem.at[0, half, offset],
            recv_sem=ag_sem.at[1, half, offset],
            device_id={"ga": peer(offset)},
            device_id_type=MESH,
        )

    def residual(half):
        for offset in (1, 3, 2):
            part_copy(half, offset).wait()
        attn = part_out[half, 0] + part_in[half, 1] + part_in[half, 2] + part_in[half, 3]
        own = pl.ds(pl.multiple_of(group * QUARTER, QUARTER), QUARTER)
        held = tokens[32 * half : 32 * half + 32, own].astype(F32)
        resid[half, group] = (held + attn).astype(BF16)
        for offset in (2, 1, 3):
            quarter_copy(half, offset, group).start()

    pending = score(0)
    for batch in range(REQUESTS // BATCH):
        following = score(batch + 1) if batch < 3 else None
        mix(batch, *pending)
        pending = following
        if batch == 1:
            project(0)
    project(1)
    residual(0)

    hit = jnp.zeros((TOKENS, EXPERTS), F32)
    expert_of = iota((EXPERTS, REQUESTS), 0)
    row, col = iota((TOKENS, REQUESTS), 0), iota((TOKENS, REQUESTS), 1)
    for draft in range(2):
        named = routes_ref[draft, 0:1] == expert_of
        for choice in range(1, 8):
            named = named | (routes_ref[draft, choice : choice + 1] == expert_of)
        hit = hit + dot_nt(one_hot(row == 2 * col + draft), one_hot(named))
    hit = hit > 0.5
    earlier = one_hot(iota((TOKENS, TOKENS), 0) > iota((TOKENS, TOKENS), 1))
    slots = dot(earlier, one_hot(hit))
    code = jnp.where(hit, slots, -1.0).astype(BF16)
    code_a = jnp.concatenate([code] * 2, axis=0)
    code_b = jnp.concatenate([code] * 8, axis=0)
    base = group * N_MEMBERS
    spread = one_hot(
        other(iota((ROWS, EXPERTS), 0) // 16) + base == iota((ROWS, EXPERTS), 1)
    )
    row, col = iota((ROWS, 2 * TOKENS), 0), iota((ROWS, 2 * TOKENS), 1)
    sel_a[...] = one_hot(
        (dot_nt(spread, code_a) == (row % 8).astype(F32)) & ((row // 8) % 2 == col // TOKENS)
    )
    row, col = iota((ROWS, 8 * TOKENS), 0), iota((ROWS, 8 * TOKENS), 1)
    sel_b[...] = one_hot(
        (dot_nt(spread, code_b) == (8 + row % 2).astype(F32)) & ((row // 2) % 8 == col // TOKENS)
    )
    residual(1)
    for half in range(2):
        for offset in (1, 3, 2):
            quarter_copy(half, offset, group).wait_send()
            quarter_copy(half, offset, peer(N_GROUPS - offset)).wait_recv()
        here = slice(32 * half, 32 * half + 32)
        squares = jnp.zeros((32, 1), F32)
        for quarter in range(N_GROUPS):
            values = resid[half, quarter].astype(F32)
            squares = squares + jnp.sum(values * values, axis=-1, keepdims=True)
        scale = lax.rsqrt(squares / WIDTH + NORM_EPS)
        for quarter in range(N_GROUPS):
            mid[here, quarter * QUARTER : (quarter + 1) * QUARTER] = (
                resid[half, quarter].astype(F32) * scale
            ).astype(BF16)

    def exchange(half, outward, source, middle, final, first_sem, second_sem):
        at = other if outward else mirror
        source, middle, final = source.at[half], middle.at[half], final.at[half]

        def copy(src, dst, sem, index, offset):
            return pltpu.make_async_remote_copy(
                src_ref=src,
                dst_ref=dst,
                send_sem=sem.at[half, 0, index],
                recv_sem=sem.at[half, 1, index],
                device_id={"dev": at(offset)},
                device_id_type=MESH,
            )

        def along_x(dx):
            return copy(source.at[dx, 0], middle.at[dx, 0], first_sem, dx, 8 * dx)

        def along_z(dz):
            return copy(source.at[:, 1, dz], middle.at[:, 1, dz], first_sem, 4 + dz, 4 + dz)

        def then_z(dx, dz):
            origin = source if dx == 0 else middle
            return copy(origin.at[dx, 0, dz], final.at[dx, 0, dz], second_sem, 8 * dx + dz, dz)

        def then_x(dx, dz):
            origin, place = middle.at[dx, 1, dz], final.at[dx, 1, dz]
            return copy(origin, place, second_sem, 8 * dx + 4 + dz, 8 * dx)

        def start():
            for dx, dz in ((2, 2), (1, 1), (3, 3)):
                along_x(dx).start()
                along_z(dz).start()
            along_z(0).start()
            for dz in (2, 1, 3):
                then_z(0, dz).start()

        def forward():
            along_z(0).wait()
            for dx in (2, 1, 3):
                then_x(dx, 0).start()
            for dx, dz in ((1, 1), (3, 3), (2, 2)):
                along_x(dx).wait()
                for far in (2, 1, 3):
                    then_z(dx, far).start()
                along_z(dz).wait()
                for far in (2, 1, 3):
                    then_x(far, dz).start()
            final[0, 0, 0] = source[0, 0, 0]
            for place in range(1, 4):
                final[place, 0, 0] = middle[place, 0, 0]
            for place in range(4):
                final[0, 1, place] = middle[0, 1, place]

        def finish():
            for dx in range(4):
                for dz in range(4):
                    if dz:
                        then_z(dx, dz).wait()
                    if dx:
                        then_x(dx, dz).wait()

        return start, forward, finish

    going = []
    for half in range(2):
        pieces = [
            mid[:, quarter * QUARTER + 256 * half : quarter * QUARTER + 256 * half + 256]
            for quarter in range(N_GROUPS)
        ]
        wide = [jnp.concatenate(pieces[2 * k : 2 * k + 2], axis=1) for k in range(2)]
        packed = dot(sel_a[...], jnp.concatenate(wide, axis=0)).astype(BF16)
        send[half, :, :, :, :, :512] = packed.reshape(4, 2, 4, 16, 512)
        narrow = [pieces[k // 2][:, 128 * (k % 2) : 128 * (k % 2) + 128] for k in range(8)]
        packed = dot(sel_b[...], jnp.concatenate(narrow, axis=0)).astype(BF16)
        send[half, :, :, :, :, 512:] = packed.reshape(4, 2, 4, 16, 128)
        going.append(
            exchange(half, True, send, relay, recv, go_first, go_second)
        )
        going[half][0]()
    going[0][1]()
    going[1][1]()

    row, col = iota((ROWS, ROWS), 0), iota((ROWS, ROWS), 1)
    unpack = one_hot(((row % 64) // 2) * 16 + (row // 64) * 2 + row % 2 == col)
    pack = one_hot(((col % 64) // 2) * 16 + (col // 64) * 2 + col % 2 == row)

    for load in load_gate_up:
        load.wait()
    load_down.wait()

    for half in range(2):
        going[half][2]()
        got = recv[half, :, :, :, :, :512].reshape(N_MEMBERS, 16, 512).astype(F32)
        last = recv[half, :, :, :, :, 512:].reshape(ROWS, 128)
        last = dot(unpack, last).astype(BF16)
        for quarter in range(N_GROUPS):
            k, place = quarter // 2, 256 * (quarter % 2)
            start = 256 * quarter
            rows[:256, start : start + 256] = (
                got[:, 8 * k : 8 * k + 8, place : place + 256].reshape(256, 256).astype(BF16)
            )
            for j in range(2):
                at = 64 * (2 * quarter + j)
                rows[256:, start + 128 * j : start + 128 * j + 128] = last[at : at + 64]
        for chunk in range(6):
            columns = slice(256 * chunk, 256 * chunk + 256)
            product = dot(rows[...], gate_up[half, :, columns])
            if half == 0:
                inner_sums[:, columns] = product
            else:
                inner_sums[:, columns] += product
    gate = inner_sums[:, :FF]
    acts[...] = (gate / (1.0 + jnp.exp(-gate)) * inner_sums[:, FF:]).astype(BF16)
    coming = []
    for half in range(2):
        for quarter in range(N_GROUPS):
            k, place = quarter // 2, 256 * (quarter % 2)
            start = quarter * QUARTER + 256 * half
            result = dot(acts[...], down[:, start : start + 256])
            back[half, :, :, :, 8 * k : 8 * k + 8, place : place + 256] = (
                result[:256].astype(BF16).reshape(4, 2, 4, 8, 256)
            )
            for j in range(2):
                at = 64 * (2 * quarter + j)
                made[at : at + 64] = result[256:, 128 * j : 128 * j + 128].astype(BF16)
        back[half, :, :, :, :, 512:] = (
            dot(pack, made[...]).astype(BF16).reshape(4, 2, 4, 16, 128)
        )
        coming.append(
            exchange(half, False, back, back_relay, home, back_first, back_second)
        )
        coming[half][0]()
    gather = one_hot(
        other(iota((EXPERTS, ROWS), 1) // 16) + base == iota((EXPERTS, ROWS), 0)
    )
    row, col = iota((2 * TOKENS, ROWS), 0), iota((2 * TOKENS, ROWS), 1)
    mask_a = (dot(code_a, gather) == (col % 8).astype(F32)) & ((col // 8) % 2 == row // TOKENS)
    row, col = iota((8 * TOKENS, ROWS), 0), iota((8 * TOKENS, ROWS), 1)
    mask_b = (dot(code_b, gather) == (8 + col % 2).astype(F32)) & ((col // 2) % 8 == row // TOKENS)

    logits = dot(mid[...], router_ref[...])
    top = jnp.max(jnp.where(hit, logits, -jnp.inf), axis=-1, keepdims=True)
    raised = jnp.where(hit, jnp.exp(logits - top), 0.0)
    gates = raised / jnp.sum(raised, axis=-1, keepdims=True)
    rest = gates
    for term in range(3):
        piece = rest.astype(BF16)
        rest = rest - piece.astype(F32)
        spread_a = dot(jnp.concatenate([piece] * 2, axis=0), gather)
        comb = jnp.where(mask_a, spread_a, 0.0).astype(BF16)
        for k in range(2):
            comb_a[k, term * TOKENS : (term + 1) * TOKENS] = comb[k * TOKENS : (k + 1) * TOKENS]
        spread_b = dot(jnp.concatenate([piece] * 8, axis=0), gather)
        comb = jnp.where(mask_b, spread_b, 0.0).astype(BF16)
        for k in range(8):
            comb_b[k, term * TOKENS : (term + 1) * TOKENS] = comb[k * TOKENS : (k + 1) * TOKENS]
    coming[0][1]()
    coming[1][1]()

    def moe_copy(half, offset):
        return pltpu.make_async_remote_copy(
            src_ref=moe_out.at[half, offset],
            dst_ref=moe_in.at[half, offset],
            send_sem=fin_sem.at[0, half, offset],
            recv_sem=fin_sem.at[1, half, offset],
            device_id={"ga": peer(offset)},
            device_id_type=MESH,
        )

    for half in range(2):
        coming[half][2]()
        for offset in order:
            quarter = peer(offset)
            place = pl.ds(pl.multiple_of((quarter % 2) * 256, 256), 256)
            wide = home[half, :, :, :, :, place].reshape(ROWS, 256)
            summed = dot(comb_a[quarter // 2], wide)
            last = home[half, :, :, :, :, 512:].reshape(ROWS, 128)
            more = [dot(comb_b[2 * quarter + j], last) for j in range(2)]
            summed = summed + jnp.concatenate(more, axis=1)
            moe_out[half, offset] = (
                summed[:TOKENS] + summed[TOKENS : 2 * TOKENS] + summed[2 * TOKENS :]
            )
            if offset:
                moe_copy(half, offset).start()
    base = jnp.concatenate([resid[0, group], resid[1, group]], axis=0).astype(F32)
    for half in range(2):
        columns = slice(256 * half, 256 * half + 256)
        for offset in (1, 3, 2):
            moe_copy(half, offset).wait()
        moe = moe_out[half, 0] + moe_in[half, 1] + moe_in[half, 2] + moe_in[half, 3]
        final = base[:, columns] + moe
        out_ref[:, :, columns] = final.reshape(REQUESTS, 2, 256).astype(BF16)


def layer(lengths, hidden, w_router, routes, w_qkv, cache, w_out, gate_up, down):
    exponent = np.arange(HD // 2) * (2.0 / HD)
    speeds = np.tile(ROPE_BASE**-exponent, 2).astype(np.float32)[None, :]
    smem = pl.BlockSpec(memory_space=pltpu.SMEM)
    vmem = pl.BlockSpec(memory_space=pltpu.VMEM)
    hbm = pl.BlockSpec(memory_space=pl.ANY)
    dma = pltpu.SemaphoreType.DMA
    packed = pltpu.VMEM((2, 4, 2, 4, 16, PACKED), BF16)
    parts = pltpu.VMEM((2, N_GROUPS, 32, QUARTER), F32)
    sums = pltpu.VMEM((2, N_GROUPS, TOKENS, 256), F32)
    return pl.pallas_call(
        layer_kernel,
        out_shape=jax.ShapeDtypeStruct((REQUESTS, 2, QUARTER), BF16),
        in_specs=[smem] + [vmem] * 4 + [hbm] * 5,
        out_specs=vmem,
        scratch_shapes=[
            pltpu.VMEM((5, WIDTH, 256), BF16),
            pltpu.VMEM((REQUESTS, 2, CONTEXT, HD), BF16),
            pltpu.VMEM((TOKENS, WIDTH), BF16),
            pltpu.VMEM((ROWS, HD), BF16),
            pltpu.VMEM((N_GROUPS, 1024, QUARTER), BF16),
            pltpu.VMEM((2, WIDTH // 2, 2 * FF), BF16),
            pltpu.VMEM((FF, WIDTH), BF16),
            parts,
            parts,
            pltpu.VMEM((2, N_GROUPS, 32, QUARTER), BF16),
            pltpu.VMEM((TOKENS, WIDTH), BF16),
            pltpu.VMEM((ROWS, 2 * TOKENS), BF16),
            pltpu.VMEM((ROWS, 8 * TOKENS), BF16),
            pltpu.VMEM((2, 3 * TOKENS, ROWS), BF16),
            pltpu.VMEM((8, 3 * TOKENS, ROWS), BF16),
            packed,
            packed,
            packed,
            packed,
            packed,
            packed,
            pltpu.VMEM((320, WIDTH // 2), BF16),
            pltpu.VMEM((320, 2 * FF), F32),
            pltpu.VMEM((320, FF), BF16),
            pltpu.VMEM((ROWS, 128), BF16),
            sums,
            sums,
            dma((5,)),
            dma((REQUESTS // BATCH,)),
            dma((5,)),
            dma((2, N_GROUPS)),
            dma((2, 2, N_GROUPS)),
            dma((2, 2, N_GROUPS)),
            dma((2, 2, 8)),
            dma((2, 2, N_MEMBERS)),
            dma((2, 2, 8)),
            dma((2, 2, N_MEMBERS)),
            dma((2, 2, N_GROUPS)),
        ],
        compiler_params=pltpu.CompilerParams(
            collective_id=0, has_side_effects=True, vmem_limit_bytes=56 * 1024 * 1024
        ),
    )(lengths, speeds, hidden, w_router, routes, w_qkv, cache, w_out, gate_up, down)


def body(hidden_in, w_qkv, w_out, cache, lengths, w_router, routes, w_gate_up, w_down):
    return layer(
        lengths,
        hidden_in,
        w_router,
        jnp.transpose(routes, (1, 2, 0)),
        w_qkv[:, 0],
        cache[:, 0],
        w_out[0],
        w_gate_up[0],
        w_down[0],
    )


def solution(mesh):
    return jax.shard_map(
        body,
        mesh=mesh,
        in_specs=(
            P("dev", None, None),
            P(None, "ga", None),
            P("ga", None, None),
            P("dev", "ga", None, None, None),
            P("dev"),
            P(),
            P("dev", None, None),
            P(("ga", "dev"), None, None),
            P(("ga", "dev"), None, None),
        ),
        out_specs=P("dev", None, "ga"),
        check_vma=False,
    )
```

```python
import jax
import jax.numpy as jnp
import numpy as np
from jax import lax
from jax.experimental import pallas as pl
from jax.experimental.pallas import tpu as pltpu
from jax.sharding import PartitionSpec as P

ROPE_BASE = 1000000.0
NORM_EPS = 1e-06
N_GROUPS = 4
N_MEMBERS = 32
TOKENS = 64
WIDTH = 2048
QUARTER = 512
FF = 768
EXPERTS = 128
REQUESTS = 32
HD = 128
HEADS = 8
CONTEXT = 768
BATCH = 8
ROWS = 16 * N_MEMBERS
PACKED = 640
MESH = pl.DeviceIdType.MESH
F32 = jnp.float32
BF16 = jnp.bfloat16


def iota(shape, axis):
    return lax.broadcasted_iota(jnp.int32, shape, axis)


def dot(a, b):
    return jnp.dot(a, b, preferred_element_type=F32)


def dot_nt(a, b):
    return lax.dot_general(a, b, (((1,), (1,)), ((), ())), preferred_element_type=F32)


def one_hot(mask):
    return jnp.where(mask, 1.0, 0.0).astype(BF16)


def layer_kernel(
    lengths_hbm,
    hidden_hbm,
    router_hbm,
    routes_hbm,
    w_qkv_hbm,
    cache_hbm,
    w_out_hbm,
    gate_up_hbm,
    down_hbm,
    out_ref,
    lengths_ref,
    hidden_ref,
    router_ref,
    routes_ref,
    w_qkv,
    cache,
    tokens,
    head_out,
    w_out,
    gate_up,
    down,
    part_out,
    part_in,
    resid,
    mid,
    sel_a,
    sel_b,
    comb_a,
    comb_b,
    send,
    relay,
    recv,
    back,
    back_relay,
    home,
    rows,
    inner_sums,
    acts,
    made,
    moe_out,
    moe_in,
    small_sem,
    qkv_sem,
    cache_sem,
    load_sem,
    gate_sem,
    rs_sem,
    ag_sem,
    go_first,
    go_second,
    back_first,
    back_second,
    fin_sem,
):
    group = lax.axis_index("ga")
    member = lax.axis_index("dev")
    x, z, core = member // 8, (member // 2) % 4, member % 2

    def peer(offset):
        return lax.rem(group + offset, N_GROUPS)

    def other(offset):
        return (
            ((x + offset // 8) % 4) * 8
            + ((z + offset % 4) % 4) * 2
            + (core + (offset // 4) % 2) % 2
        )

    def mirror(offset):
        return (
            ((x + 4 - offset // 8) % 4) * 8
            + ((z + 4 - offset % 4) % 4) * 2
            + (core + (offset // 4) % 2) % 2
        )

    small_loads = [
        pltpu.make_async_copy(source, target, small_sem.at[place])
        for place, (source, target) in enumerate(
            (
                (hidden_hbm, hidden_ref),
                (lengths_hbm, lengths_ref),
                (routes_hbm, routes_ref),
                (router_hbm, router_ref),
            )
        )
    ]
    for load in small_loads[:3]:
        load.start()
    qkv_loads = [
        pltpu.make_async_copy(
            w_qkv_hbm.at[:, pl.ds(256 * chunk, 256)], w_qkv.at[chunk], qkv_sem.at[chunk]
        )
        for chunk in range(5)
    ]
    for load in qkv_loads:
        load.start()

    def cache_load(batch):
        block = pl.ds(batch * BATCH, BATCH)
        return pltpu.make_async_copy(
            cache_hbm.at[block], cache.at[block], cache_sem.at[batch]
        )

    cache_load(0).start()
    cache_load(1).start()
    order = (2, 1, 3, 0)
    loads = {}
    for offset in order:
        columns = pl.ds(pl.multiple_of(peer(offset) * QUARTER, QUARTER), QUARTER)
        loads[offset] = pltpu.make_async_copy(
            w_out_hbm.at[:, columns], w_out.at[offset], load_sem.at[offset]
        )
        loads[offset].start()
    cache_load(2).start()
    cache_load(3).start()
    small_loads[3].start()
    load_gate_up = [
        pltpu.make_async_copy(
            gate_up_hbm.at[pl.ds(QUARTER * quarter + 256 * half, 256)],
            gate_up.at[half, pl.ds(256 * quarter, 256)],
            gate_sem.at[half, quarter],
        )
        for half in range(2)
        for quarter in range(N_GROUPS)
    ]
    load_down = pltpu.make_async_copy(down_hbm, down, load_sem.at[4])

    barrier = pltpu.get_barrier_semaphore()
    for offset in range(1, N_GROUPS):
        pl.semaphore_signal(
            barrier, inc=1, device_id={"ga": peer(offset)}, device_id_type=MESH
        )
    for offset in list(range(1, 8)) + [8, 16, 24]:
        pl.semaphore_signal(
            barrier, inc=1, device_id={"dev": other(offset)}, device_id_type=MESH
        )

    for load in small_loads[:3]:
        load.wait()
    row = iota((TOKENS, HD), 0)
    places = (row % 2).astype(F32)
    for request in range(REQUESTS):
        length = lengths_ref[request].astype(F32)
        places = places + jnp.where(row // 2 == request, length, 0.0)
    speed_of = iota((1, HD), 1) % (HD // 2)
    speeds = jnp.zeros((1, HD), F32)
    for index in range(HD // 2):
        speed = float(np.float32(ROPE_BASE ** (-2.0 * index / HD)))
        speeds = jnp.where(speed_of == index, speed, speeds)
    angles = places * speeds
    cosine = jnp.cos(angles)
    sine = jnp.sin(angles)
    sine = jnp.where(iota((TOKENS, HD), 1) < HD // 2, -sine, sine)

    def rotate(values):
        return (values * cosine + pltpu.roll(values, HD // 2, 1) * sine).astype(BF16)

    hidden = hidden_ref[...].astype(F32).reshape(TOKENS, WIDTH)
    tokens[...] = hidden.astype(BF16)
    scale = lax.rsqrt(jnp.mean(hidden * hidden, axis=-1, keepdims=True) + NORM_EPS)
    normed = (hidden * scale).astype(BF16)

    stacked = []
    for chunk in range(4):
        qkv_loads[chunk].wait()
        projected = dot(normed, w_qkv[chunk])
        stacked += [rotate(projected[:, :HD]), rotate(projected[:, HD:])]
    row, col = iota((ROWS, ROWS), 0), iota((ROWS, ROWS), 1)
    by_request = one_hot(((row // 2) % 8) * TOKENS + (row // 16) * 2 + row % 2 == col)
    row, col = iota((256, 256), 0), iota((256, 256), 1)
    by_head = one_hot(((col // 2) % 8) * 32 + (col // 16) * 2 + col % 2 == row)
    queries = dot(by_request, jnp.concatenate(stacked, axis=0))
    qkv_loads[4].wait()
    projected = dot(normed, w_qkv[4])
    new_keys = rotate(projected[:, :HD])
    new_values = projected[:, HD:].astype(BF16)

    lane = iota((1, HD), 1)
    owner = iota((HD, HD), 1) // 16
    spot = iota((CONTEXT, HD), 0)
    row, col = iota((16, HD), 0), iota((16, HD), 1)
    visible = (row // 2 == col // 16) & (row % 2 <= col % 2)

    def score(batch):
        cache_load(batch).wait()
        first = batch * BATCH
        turned = queries[128 * batch : 128 * batch + 128].T
        blocks = [
            jnp.where(owner == inner, turned, 0.0).astype(BF16) for inner in range(BATCH)
        ]
        wide = jnp.concatenate(blocks, axis=0)
        scores = [
            dot(
                jnp.concatenate(
                    [cache[first + inner, 0, part : part + 256] for inner in range(BATCH)], axis=1
                ),
                wide,
            )
            for part in range(0, CONTEXT, 256)
        ]
        scores = jnp.concatenate(scores, axis=0)
        fresh = dot(new_keys[16 * batch : 16 * batch + 16], turned.astype(BF16))
        return scores, fresh

    def mix(batch, scores, fresh):
        first = batch * BATCH
        limits = jnp.zeros((1, HD), jnp.int32)
        for inner in range(BATCH):
            limits = jnp.where(lane // 16 == inner, lengths_ref[first + inner], limits)
        scores = jnp.where(spot < limits, scores * HD**-0.5, -jnp.inf)
        fresh = jnp.where(visible, fresh * HD**-0.5, -jnp.inf)
        top = jnp.maximum(
            jnp.max(scores, axis=0, keepdims=True), jnp.max(fresh, axis=0, keepdims=True)
        )
        old_exp = jnp.exp(scores - top)
        new_exp = jnp.exp(fresh - top)
        totals = jnp.sum(old_exp, axis=0, keepdims=True) + jnp.sum(
            new_exp, axis=0, keepdims=True
        )
        totals = jnp.broadcast_to(totals, (HD, HD)).T
        weights = old_exp.astype(BF16).T
        mixed = [
            dot(weights[16 * inner : 16 * inner + 16], cache[first + inner, 1])
            for inner in range(BATCH)
        ]
        mixed = jnp.concatenate(mixed, axis=0) + dot(
            new_exp.T.astype(BF16), new_values[16 * batch : 16 * batch + 16]
        )
        head_out[128 * batch : 128 * batch + 128] = (mixed / totals).astype(BF16)

    def part_copy(half, offset):
        return pltpu.make_async_remote_copy(
            src_ref=part_out.at[half, offset],
            dst_ref=part_in.at[half, offset],
            send_sem=rs_sem.at[0, half, offset],
            recv_sem=rs_sem.at[1, half, offset],
            device_id={"ga": peer(offset)},
            device_id_type=MESH,
        )

    def project(half):
        by_heads = dot(by_head, head_out[256 * half : 256 * half + 256]).astype(BF16)
        heads = jnp.concatenate(
            [by_heads[32 * head : 32 * head + 32] for head in range(HEADS)], axis=1
        )
        for place, offset in enumerate(order):
            if half == 0:
                loads[offset].wait()
            part_out[half, offset] = dot(heads, w_out[offset])
            if half == 0 and place == 0:
                pl.semaphore_wait(barrier, 13)
            if offset:
                part_copy(half, offset).start()

    def quarter_copy(half, offset, place):
        return pltpu.make_async_remote_copy(
            src_ref=resid.at[half, group],
            dst_ref=resid.at[half, place],
            send_sem=ag_sem.at[0, half, offset],
            recv_sem=ag_sem.at[1, half, offset],
            device_id={"ga": peer(offset)},
            device_id_type=MESH,
        )

    def residual(half):
        for offset in (1, 3, 2):
            part_copy(half, offset).wait()
        attn = part_out[half, 0] + part_in[half, 1] + part_in[half, 2] + part_in[half, 3]
        own = pl.ds(pl.multiple_of(group * QUARTER, QUARTER), QUARTER)
        held = tokens[32 * half : 32 * half + 32, own].astype(F32)
        resid[half, group] = (held + attn).astype(BF16)
        for offset in (2, 1, 3):
            quarter_copy(half, offset, group).start()

    pending = score(0)
    for batch in range(REQUESTS // BATCH):
        following = score(batch + 1) if batch < 3 else None
        mix(batch, *pending)
        pending = following
        if batch == 1:
            project(0)
    for load in load_gate_up:
        load.start()
    load_down.start()
    project(1)
    residual(0)

    hit = jnp.zeros((TOKENS, EXPERTS), F32)
    expert_of = iota((EXPERTS, REQUESTS), 0)
    row, col = iota((TOKENS, REQUESTS), 0), iota((TOKENS, REQUESTS), 1)
    for draft in range(2):
        named = routes_ref[draft, 0:1] == expert_of
        for choice in range(1, 8):
            named = named | (routes_ref[draft, choice : choice + 1] == expert_of)
        hit = hit + dot_nt(one_hot(row == 2 * col + draft), one_hot(named))
    hit = hit > 0.5
    earlier = one_hot(iota((TOKENS, TOKENS), 0) > iota((TOKENS, TOKENS), 1))
    slots = dot(earlier, one_hot(hit))
    code = jnp.where(hit, slots, -1.0).astype(BF16)
    code_a = jnp.concatenate([code] * 2, axis=0)
    code_b = jnp.concatenate([code] * 8, axis=0)
    base = group * N_MEMBERS
    spread = one_hot(
        other(iota((ROWS, EXPERTS), 0) // 16) + base == iota((ROWS, EXPERTS), 1)
    )
    row, col = iota((ROWS, 2 * TOKENS), 0), iota((ROWS, 2 * TOKENS), 1)
    sel_a[...] = one_hot(
        (dot_nt(spread, code_a) == (row % 8).astype(F32)) & ((row // 8) % 2 == col // TOKENS)
    )
    row, col = iota((ROWS, 8 * TOKENS), 0), iota((ROWS, 8 * TOKENS), 1)
    sel_b[...] = one_hot(
        (dot_nt(spread, code_b) == (8 + row % 2).astype(F32)) & ((row // 2) % 8 == col // TOKENS)
    )
    residual(1)
    for half in range(2):
        for offset in (1, 3, 2):
            quarter_copy(half, offset, group).wait_send()
            quarter_copy(half, offset, peer(N_GROUPS - offset)).wait_recv()
        here = slice(32 * half, 32 * half + 32)
        squares = jnp.zeros((32, 1), F32)
        for quarter in range(N_GROUPS):
            values = resid[half, quarter].astype(F32)
            squares = squares + jnp.sum(values * values, axis=-1, keepdims=True)
        scale = lax.rsqrt(squares / WIDTH + NORM_EPS)
        for quarter in range(N_GROUPS):
            mid[here, quarter * QUARTER : (quarter + 1) * QUARTER] = (
                resid[half, quarter].astype(F32) * scale
            ).astype(BF16)

    def exchange(half, outward, source, middle, final, first_sem, second_sem):
        at = other if outward else mirror
        source, middle, final = source.at[half], middle.at[half], final.at[half]

        def copy(src, dst, sem, index, offset):
            return pltpu.make_async_remote_copy(
                src_ref=src,
                dst_ref=dst,
                send_sem=sem.at[half, 0, index],
                recv_sem=sem.at[half, 1, index],
                device_id={"dev": at(offset)},
                device_id_type=MESH,
            )

        def along_x(dx):
            return copy(source.at[dx, 0], middle.at[dx, 0], first_sem, dx, 8 * dx)

        def along_z(dz):
            return copy(source.at[:, 1, dz], middle.at[:, 1, dz], first_sem, 4 + dz, 4 + dz)

        def then_z(dx, dz):
            origin = source if dx == 0 else middle
            return copy(origin.at[dx, 0, dz], final.at[dx, 0, dz], second_sem, 8 * dx + dz, dz)

        def then_x(dx, dz):
            origin, place = middle.at[dx, 1, dz], final.at[dx, 1, dz]
            return copy(origin, place, second_sem, 8 * dx + 4 + dz, 8 * dx)

        def start():
            for dx, dz in ((2, 2), (1, 1), (3, 3)):
                along_x(dx).start()
                along_z(dz).start()
            along_z(0).start()

        def forward():
            along_z(0).wait()
            for dx in (2, 1, 3):
                then_x(dx, 0).start()
            for dx, dz in ((1, 1), (3, 3), (2, 2)):
                along_x(dx).wait()
                for far in (2, 1, 3):
                    then_z(dx, far).start()
                along_z(dz).wait()
                for far in (2, 1, 3):
                    then_x(far, dz).start()
            for dz in (2, 1, 3):
                then_z(0, dz).start()
            final[0, 0, 0] = source[0, 0, 0]
            for place in range(1, 4):
                final[place, 0, 0] = middle[place, 0, 0]
            for place in range(4):
                final[0, 1, place] = middle[0, 1, place]

        def finish():
            for dx in range(4):
                for dz in range(4):
                    if dz:
                        then_z(dx, dz).wait()
                    if dx:
                        then_x(dx, dz).wait()

        return start, forward, finish

    going = []
    for half in range(2):
        pieces = [
            mid[:, quarter * QUARTER + 256 * half : quarter * QUARTER + 256 * half + 256]
            for quarter in range(N_GROUPS)
        ]
        wide = [jnp.concatenate(pieces[2 * k : 2 * k + 2], axis=1) for k in range(2)]
        packed = dot(sel_a[...], jnp.concatenate(wide, axis=0)).astype(BF16)
        send[half, :, :, :, :, :512] = packed.reshape(4, 2, 4, 16, 512)
        narrow = [pieces[k // 2][:, 128 * (k % 2) : 128 * (k % 2) + 128] for k in range(8)]
        packed = dot(sel_b[...], jnp.concatenate(narrow, axis=0)).astype(BF16)
        send[half, :, :, :, :, 512:] = packed.reshape(4, 2, 4, 16, 128)
        going.append(
            exchange(half, True, send, relay, recv, go_first, go_second)
        )
        going[half][0]()
    going[0][1]()
    going[1][1]()

    row, col = iota((ROWS, ROWS), 0), iota((ROWS, ROWS), 1)
    unpack = one_hot(((row % 64) // 2) * 16 + (row // 64) * 2 + row % 2 == col)
    pack = one_hot(((col % 64) // 2) * 16 + (col // 64) * 2 + col % 2 == row)

    for load in load_gate_up:
        load.wait()
    load_down.wait()

    for half in range(2):
        going[half][2]()
        got = recv[half, :, :, :, :, :512].reshape(N_MEMBERS, 16, 512).astype(F32)
        last = recv[half, :, :, :, :, 512:].reshape(ROWS, 128)
        last = dot(unpack, last).astype(BF16)
        for quarter in range(N_GROUPS):
            k, place = quarter // 2, 256 * (quarter % 2)
            start = 256 * quarter
            rows[:256, start : start + 256] = (
                got[:, 8 * k : 8 * k + 8, place : place + 256].reshape(256, 256).astype(BF16)
            )
            for j in range(2):
                at = 64 * (2 * quarter + j)
                rows[256:, start + 128 * j : start + 128 * j + 128] = last[at : at + 64]
        for chunk in range(6):
            columns = slice(256 * chunk, 256 * chunk + 256)
            product = dot(rows[...], gate_up[half, :, columns])
            if half == 0:
                inner_sums[:, columns] = product
            else:
                inner_sums[:, columns] += product
    gate = inner_sums[:, :FF]
    acts[...] = (gate / (1.0 + jnp.exp(-gate)) * inner_sums[:, FF:]).astype(BF16)
    coming = []
    for half in range(2):
        for quarter in range(N_GROUPS):
            k, place = quarter // 2, 256 * (quarter % 2)
            start = quarter * QUARTER + 256 * half
            result = dot(acts[...], down[:, start : start + 256])
            back[half, :, :, :, 8 * k : 8 * k + 8, place : place + 256] = (
                result[:256].astype(BF16).reshape(4, 2, 4, 8, 256)
            )
            for j in range(2):
                at = 64 * (2 * quarter + j)
                made[at : at + 64] = result[256:, 128 * j : 128 * j + 128].astype(BF16)
        back[half, :, :, :, :, 512:] = (
            dot(pack, made[...]).astype(BF16).reshape(4, 2, 4, 16, 128)
        )
        coming.append(
            exchange(half, False, back, back_relay, home, back_first, back_second)
        )
        coming[half][0]()
    gather = one_hot(
        other(iota((EXPERTS, ROWS), 1) // 16) + base == iota((EXPERTS, ROWS), 0)
    )
    row, col = iota((2 * TOKENS, ROWS), 0), iota((2 * TOKENS, ROWS), 1)
    mask_a = (dot(code_a, gather) == (col % 8).astype(F32)) & ((col // 8) % 2 == row // TOKENS)
    row, col = iota((8 * TOKENS, ROWS), 0), iota((8 * TOKENS, ROWS), 1)
    mask_b = (dot(code_b, gather) == (8 + col % 2).astype(F32)) & ((col // 2) % 8 == row // TOKENS)

    small_loads[3].wait()
    logits = dot(mid[...], router_ref[...])
    top = jnp.max(jnp.where(hit, logits, -jnp.inf), axis=-1, keepdims=True)
    raised = jnp.where(hit, jnp.exp(logits - top), 0.0)
    gates = raised / jnp.sum(raised, axis=-1, keepdims=True)
    rest = gates
    for term in range(3):
        piece = rest.astype(BF16)
        rest = rest - piece.astype(F32)
        spread_a = dot(jnp.concatenate([piece] * 2, axis=0), gather)
        comb = jnp.where(mask_a, spread_a, 0.0).astype(BF16)
        for k in range(2):
            comb_a[k, term * TOKENS : (term + 1) * TOKENS] = comb[k * TOKENS : (k + 1) * TOKENS]
        spread_b = dot(jnp.concatenate([piece] * 8, axis=0), gather)
        comb = jnp.where(mask_b, spread_b, 0.0).astype(BF16)
        for k in range(8):
            comb_b[k, term * TOKENS : (term + 1) * TOKENS] = comb[k * TOKENS : (k + 1) * TOKENS]
    coming[0][1]()
    coming[1][1]()

    def moe_copy(half, offset):
        return pltpu.make_async_remote_copy(
            src_ref=moe_out.at[half, offset],
            dst_ref=moe_in.at[half, offset],
            send_sem=fin_sem.at[0, half, offset],
            recv_sem=fin_sem.at[1, half, offset],
            device_id={"ga": peer(offset)},
            device_id_type=MESH,
        )

    for half in range(2):
        coming[half][2]()
        for offset in order:
            quarter = peer(offset)
            place = pl.ds(pl.multiple_of((quarter % 2) * 256, 256), 256)
            wide = home[half, :, :, :, :, place].reshape(ROWS, 256)
            summed = dot(comb_a[quarter // 2], wide)
            last = home[half, :, :, :, :, 512:].reshape(ROWS, 128)
            more = [dot(comb_b[2 * quarter + j], last) for j in range(2)]
            summed = summed + jnp.concatenate(more, axis=1)
            moe_out[half, offset] = (
                summed[:TOKENS] + summed[TOKENS : 2 * TOKENS] + summed[2 * TOKENS :]
            )
            if offset:
                moe_copy(half, offset).start()
    base = jnp.concatenate([resid[0, group], resid[1, group]], axis=0).astype(F32)
    for half in range(2):
        columns = slice(256 * half, 256 * half + 256)
        for offset in (1, 3, 2):
            moe_copy(half, offset).wait()
        moe = moe_out[half, 0] + moe_in[half, 1] + moe_in[half, 2] + moe_in[half, 3]
        final = base[:, columns] + moe
        out_ref[:, :, columns] = final.reshape(REQUESTS, 2, 256).astype(BF16)


def layer(lengths, hidden, w_router, routes, w_qkv, cache, w_out, gate_up, down):
    vmem = pl.BlockSpec(memory_space=pltpu.VMEM)
    hbm = pl.BlockSpec(memory_space=pl.ANY)
    dma = pltpu.SemaphoreType.DMA
    packed = pltpu.VMEM((2, 4, 2, 4, 16, PACKED), BF16)
    parts = pltpu.VMEM((2, N_GROUPS, 32, QUARTER), F32)
    sums = pltpu.VMEM((2, N_GROUPS, TOKENS, 256), F32)
    return pl.pallas_call(
        layer_kernel,
        out_shape=jax.ShapeDtypeStruct((REQUESTS, 2, QUARTER), BF16),
        in_specs=[hbm] * 9,
        out_specs=vmem,
        scratch_shapes=[
            pltpu.SMEM((REQUESTS,), jnp.int32),
            pltpu.VMEM((REQUESTS, 2, WIDTH), BF16),
            pltpu.VMEM((WIDTH, EXPERTS), BF16),
            pltpu.VMEM((2, 8, REQUESTS), jnp.int32),
            pltpu.VMEM((5, WIDTH, 256), BF16),
            pltpu.VMEM((REQUESTS, 2, CONTEXT, HD), BF16),
            pltpu.VMEM((TOKENS, WIDTH), BF16),
            pltpu.VMEM((ROWS, HD), BF16),
            pltpu.VMEM((N_GROUPS, 1024, QUARTER), BF16),
            pltpu.VMEM((2, WIDTH // 2, 2 * FF), BF16),
            pltpu.VMEM((FF, WIDTH), BF16),
            parts,
            parts,
            pltpu.VMEM((2, N_GROUPS, 32, QUARTER), BF16),
            pltpu.VMEM((TOKENS, WIDTH), BF16),
            pltpu.VMEM((ROWS, 2 * TOKENS), BF16),
            pltpu.VMEM((ROWS, 8 * TOKENS), BF16),
            pltpu.VMEM((2, 3 * TOKENS, ROWS), BF16),
            pltpu.VMEM((8, 3 * TOKENS, ROWS), BF16),
            packed,
            packed,
            packed,
            packed,
            packed,
            packed,
            pltpu.VMEM((320, WIDTH // 2), BF16),
            pltpu.VMEM((320, 2 * FF), F32),
            pltpu.VMEM((320, FF), BF16),
            pltpu.VMEM((ROWS, 128), BF16),
            sums,
            sums,
            dma((4,)),
            dma((5,)),
            dma((REQUESTS // BATCH,)),
            dma((5,)),
            dma((2, N_GROUPS)),
            dma((2, 2, N_GROUPS)),
            dma((2, 2, N_GROUPS)),
            dma((2, 2, 8)),
            dma((2, 2, N_MEMBERS)),
            dma((2, 2, 8)),
            dma((2, 2, N_MEMBERS)),
            dma((2, 2, N_GROUPS)),
        ],
        compiler_params=pltpu.CompilerParams(
            collective_id=0, has_side_effects=True, vmem_limit_bytes=56 * 1024 * 1024
        ),
    )(lengths, hidden, w_router, routes, w_qkv, cache, w_out, gate_up, down)


def body(hidden_in, w_qkv, w_out, cache, lengths, w_router, routes, w_gate_up, w_down):
    return layer(
        lengths,
        hidden_in,
        w_router,
        jnp.transpose(routes, (1, 2, 0)),
        w_qkv[:, 0],
        cache[:, 0],
        w_out[0],
        w_gate_up[0],
        w_down[0],
    )


def solution(mesh):
    return jax.shard_map(
        body,
        mesh=mesh,
        in_specs=(
            P("dev", None, None),
            P(None, "ga", None),
            P("ga", None, None),
            P("dev", "ga", None, None, None),
            P("dev"),
            P(),
            P("dev", None, None),
            P(("ga", "dev"), None, None),
            P(("ga", "dev"), None, None),
        ),
        out_specs=P("dev", None, "ga"),
        check_vma=False,
    )
```

```python
import jax
import jax.numpy as jnp
import numpy as np
from jax import lax
from jax.experimental import pallas as pl
from jax.experimental.pallas import tpu as pltpu
from jax.sharding import PartitionSpec as P

ROPE_BASE = 1000000.0
NORM_EPS = 1e-06
N_GROUPS = 4
N_MEMBERS = 32
TOKENS = 64
WIDTH = 2048
QUARTER = 512
FF = 768
EXPERTS = 128
REQUESTS = 32
HD = 128
HEADS = 8
CONTEXT = 768
BATCH = 8
ROWS = 16 * N_MEMBERS
PACKED = 640
MESH = pl.DeviceIdType.MESH
F32 = jnp.float32
BF16 = jnp.bfloat16


def iota(shape, axis):
    return lax.broadcasted_iota(jnp.int32, shape, axis)


def dot(a, b):
    return jnp.dot(a, b, preferred_element_type=F32)


def dot_nt(a, b):
    return lax.dot_general(a, b, (((1,), (1,)), ((), ())), preferred_element_type=F32)


def one_hot(mask):
    return jnp.where(mask, 1.0, 0.0).astype(BF16)


def layer_kernel(
    lengths_hbm,
    hidden_hbm,
    router_hbm,
    routes_hbm,
    w_qkv_hbm,
    cache_hbm,
    w_out_hbm,
    gate_up_hbm,
    down_hbm,
    out_ref,
    lengths_ref,
    hidden_ref,
    router_ref,
    routes_ref,
    w_qkv,
    cache,
    tokens,
    head_out,
    w_out,
    gate_up,
    down,
    part_out,
    part_in,
    resid,
    mid,
    sel_a,
    sel_b,
    comb_a,
    comb_b,
    send,
    relay,
    recv,
    back,
    back_relay,
    home,
    rows,
    inner_sums,
    acts,
    made,
    moe_out,
    moe_in,
    small_sem,
    qkv_sem,
    cache_sem,
    load_sem,
    gate_sem,
    rs_sem,
    ag_sem,
    go_first,
    go_second,
    back_first,
    back_second,
    fin_sem,
):
    group = lax.axis_index("ga")
    member = lax.axis_index("dev")
    x, z, core = member // 8, (member // 2) % 4, member % 2

    def peer(offset):
        return lax.rem(group + offset, N_GROUPS)

    def other(offset):
        return (
            ((x + offset // 8) % 4) * 8
            + ((z + offset % 4) % 4) * 2
            + (core + (offset // 4) % 2) % 2
        )

    def mirror(offset):
        return (
            ((x + 4 - offset // 8) % 4) * 8
            + ((z + 4 - offset % 4) % 4) * 2
            + (core + (offset // 4) % 2) % 2
        )

    small_loads = [
        pltpu.make_async_copy(source, target, small_sem.at[place])
        for place, (source, target) in enumerate(
            (
                (hidden_hbm, hidden_ref),
                (lengths_hbm, lengths_ref),
                (routes_hbm, routes_ref),
                (router_hbm, router_ref),
            )
        )
    ]
    for load in small_loads[:3]:
        load.start()
    qkv_loads = [
        pltpu.make_async_copy(
            w_qkv_hbm.at[:, pl.ds(256 * chunk, 256)], w_qkv.at[chunk], qkv_sem.at[chunk]
        )
        for chunk in range(5)
    ]
    for load in qkv_loads:
        load.start()

    def cache_load(batch):
        block = pl.ds(batch * BATCH, BATCH)
        return pltpu.make_async_copy(
            cache_hbm.at[block], cache.at[block], cache_sem.at[batch]
        )

    cache_load(0).start()
    cache_load(1).start()
    order = (2, 1, 3, 0)
    loads = {}
    for offset in order:
        columns = pl.ds(pl.multiple_of(peer(offset) * QUARTER, QUARTER), QUARTER)
        loads[offset] = pltpu.make_async_copy(
            w_out_hbm.at[:, columns], w_out.at[offset], load_sem.at[offset]
        )
        loads[offset].start()
    cache_load(2).start()
    cache_load(3).start()
    small_loads[3].start()
    load_gate_up = [
        pltpu.make_async_copy(
            gate_up_hbm.at[pl.ds(QUARTER * quarter + 256 * half, 256)],
            gate_up.at[half, pl.ds(256 * quarter, 256)],
            gate_sem.at[half, quarter],
        )
        for half in range(2)
        for quarter in range(N_GROUPS)
    ]
    load_down = pltpu.make_async_copy(down_hbm, down, load_sem.at[4])

    barrier = pltpu.get_barrier_semaphore()
    for offset in range(1, N_GROUPS):
        pl.semaphore_signal(
            barrier, inc=1, device_id={"ga": peer(offset)}, device_id_type=MESH
        )
    for offset in list(range(1, 8)) + [8, 16, 24]:
        pl.semaphore_signal(
            barrier, inc=1, device_id={"dev": other(offset)}, device_id_type=MESH
        )

    for load in small_loads[:3]:
        load.wait()
    row = iota((TOKENS, HD), 0)
    places = (row % 2).astype(F32)
    for request in range(REQUESTS):
        length = lengths_ref[request].astype(F32)
        places = places + jnp.where(row // 2 == request, length, 0.0)
    speed_of = iota((1, HD), 1) % (HD // 2)
    speeds = jnp.zeros((1, HD), F32)
    for index in range(HD // 2):
        speed = float(np.float32(ROPE_BASE ** (-2.0 * index / HD)))
        speeds = jnp.where(speed_of == index, speed, speeds)
    angles = places * speeds
    cosine = jnp.cos(angles)
    sine = jnp.sin(angles)
    sine = jnp.where(iota((TOKENS, HD), 1) < HD // 2, -sine, sine)

    def rotate(values):
        return (values * cosine + pltpu.roll(values, HD // 2, 1) * sine).astype(BF16)

    hidden = hidden_ref[...].astype(F32).reshape(TOKENS, WIDTH)
    tokens[...] = hidden.astype(BF16)
    scale = lax.rsqrt(jnp.mean(hidden * hidden, axis=-1, keepdims=True) + NORM_EPS)
    normed = (hidden * scale).astype(BF16)

    stacked = []
    for chunk in range(4):
        qkv_loads[chunk].wait()
        projected = dot(normed, w_qkv[chunk])
        stacked += [rotate(projected[:, :HD]), rotate(projected[:, HD:])]
    row, col = iota((ROWS, ROWS), 0), iota((ROWS, ROWS), 1)
    by_request = one_hot(((row // 2) % 8) * TOKENS + (row // 16) * 2 + row % 2 == col)
    row, col = iota((256, 256), 0), iota((256, 256), 1)
    by_head = one_hot(((col // 2) % 8) * 32 + (col // 16) * 2 + col % 2 == row)
    queries = dot(by_request, jnp.concatenate(stacked, axis=0))
    qkv_loads[4].wait()
    projected = dot(normed, w_qkv[4])
    new_keys = rotate(projected[:, :HD])
    new_values = projected[:, HD:].astype(BF16)

    lane = iota((1, HD), 1)
    owner = iota((HD, HD), 1) // 16
    spot = iota((CONTEXT, HD), 0)
    row, col = iota((16, HD), 0), iota((16, HD), 1)
    visible = (row // 2 == col // 16) & (row % 2 <= col % 2)

    def score(batch):
        cache_load(batch).wait()
        first = batch * BATCH
        turned = queries[128 * batch : 128 * batch + 128].T
        blocks = [
            jnp.where(owner == inner, turned, 0.0).astype(BF16) for inner in range(BATCH)
        ]
        wide = jnp.concatenate(blocks, axis=0)
        scores = [
            dot(
                jnp.concatenate(
                    [cache[first + inner, 0, part : part + 256] for inner in range(BATCH)], axis=1
                ),
                wide,
            )
            for part in range(0, CONTEXT, 256)
        ]
        scores = jnp.concatenate(scores, axis=0)
        fresh = dot(new_keys[16 * batch : 16 * batch + 16], turned.astype(BF16))
        return scores, fresh

    def mix(batch, scores, fresh):
        first = batch * BATCH
        limits = jnp.zeros((1, HD), jnp.int32)
        for inner in range(BATCH):
            limits = jnp.where(lane // 16 == inner, lengths_ref[first + inner], limits)
        scores = jnp.where(spot < limits, scores * HD**-0.5, -jnp.inf)
        fresh = jnp.where(visible, fresh * HD**-0.5, -jnp.inf)
        top = jnp.maximum(
            jnp.max(scores, axis=0, keepdims=True), jnp.max(fresh, axis=0, keepdims=True)
        )
        old_exp = jnp.exp(scores - top)
        new_exp = jnp.exp(fresh - top)
        totals = jnp.sum(old_exp, axis=0, keepdims=True) + jnp.sum(
            new_exp, axis=0, keepdims=True
        )
        totals = jnp.broadcast_to(totals, (HD, HD)).T
        weights = old_exp.astype(BF16).T
        mixed = [
            dot(weights[16 * inner : 16 * inner + 16], cache[first + inner, 1])
            for inner in range(BATCH)
        ]
        mixed = jnp.concatenate(mixed, axis=0) + dot(
            new_exp.T.astype(BF16), new_values[16 * batch : 16 * batch + 16]
        )
        head_out[128 * batch : 128 * batch + 128] = (mixed / totals).astype(BF16)

    def part_copy(half, offset):
        return pltpu.make_async_remote_copy(
            src_ref=part_out.at[half, offset],
            dst_ref=part_in.at[half, offset],
            send_sem=rs_sem.at[0, half, offset],
            recv_sem=rs_sem.at[1, half, offset],
            device_id={"ga": peer(offset)},
            device_id_type=MESH,
        )

    def project(half):
        by_heads = dot(by_head, head_out[256 * half : 256 * half + 256]).astype(BF16)
        heads = jnp.concatenate(
            [by_heads[32 * head : 32 * head + 32] for head in range(HEADS)], axis=1
        )
        for place, offset in enumerate(order):
            if half == 0:
                loads[offset].wait()
            part_out[half, offset] = dot(heads, w_out[offset])
            if half == 0 and place == 0:
                pl.semaphore_wait(barrier, 13)
            if offset:
                part_copy(half, offset).start()

    def quarter_copy(half, offset, place):
        return pltpu.make_async_remote_copy(
            src_ref=resid.at[half, group],
            dst_ref=resid.at[half, place],
            send_sem=ag_sem.at[0, half, offset],
            recv_sem=ag_sem.at[1, half, offset],
            device_id={"ga": peer(offset)},
            device_id_type=MESH,
        )

    def residual(half):
        for offset in (1, 3, 2):
            part_copy(half, offset).wait()
        attn = part_out[half, 0] + part_in[half, 1] + part_in[half, 2] + part_in[half, 3]
        own = pl.ds(pl.multiple_of(group * QUARTER, QUARTER), QUARTER)
        held = tokens[32 * half : 32 * half + 32, own].astype(F32)
        resid[half, group] = (held + attn).astype(BF16)
        for offset in (2, 1, 3):
            quarter_copy(half, offset, group).start()

    pending = score(0)
    for batch in range(REQUESTS // BATCH):
        following = score(batch + 1) if batch < 3 else None
        mix(batch, *pending)
        pending = following
        if batch == 1:
            project(0)
    for load in load_gate_up:
        load.start()
    load_down.start()
    project(1)
    residual(0)

    hit = jnp.zeros((TOKENS, EXPERTS), F32)
    expert_of = iota((EXPERTS, REQUESTS), 0)
    row, col = iota((TOKENS, REQUESTS), 0), iota((TOKENS, REQUESTS), 1)
    for draft in range(2):
        named = routes_ref[draft, 0:1] == expert_of
        for choice in range(1, 8):
            named = named | (routes_ref[draft, choice : choice + 1] == expert_of)
        hit = hit + dot_nt(one_hot(row == 2 * col + draft), one_hot(named))
    hit = hit > 0.5
    earlier = one_hot(iota((TOKENS, TOKENS), 0) > iota((TOKENS, TOKENS), 1))
    slots = dot(earlier, one_hot(hit))
    code = jnp.where(hit, slots, -1.0).astype(BF16)
    code_a = jnp.concatenate([code] * 2, axis=0)
    code_b = jnp.concatenate([code] * 8, axis=0)
    base = group * N_MEMBERS
    spread = one_hot(
        other(iota((ROWS, EXPERTS), 0) // 16) + base == iota((ROWS, EXPERTS), 1)
    )
    row, col = iota((ROWS, 2 * TOKENS), 0), iota((ROWS, 2 * TOKENS), 1)
    sel_a[...] = one_hot(
        (dot_nt(spread, code_a) == (row % 8).astype(F32)) & ((row // 8) % 2 == col // TOKENS)
    )
    row, col = iota((ROWS, 8 * TOKENS), 0), iota((ROWS, 8 * TOKENS), 1)
    sel_b[...] = one_hot(
        (dot_nt(spread, code_b) == (8 + row % 2).astype(F32)) & ((row // 2) % 8 == col // TOKENS)
    )
    residual(1)
    for half in range(2):
        for offset in (1, 3, 2):
            quarter_copy(half, offset, group).wait_send()
            quarter_copy(half, offset, peer(N_GROUPS - offset)).wait_recv()
        here = slice(32 * half, 32 * half + 32)
        squares = jnp.zeros((32, 1), F32)
        for quarter in range(N_GROUPS):
            values = resid[half, quarter].astype(F32)
            squares = squares + jnp.sum(values * values, axis=-1, keepdims=True)
        scale = lax.rsqrt(squares / WIDTH + NORM_EPS)
        for quarter in range(N_GROUPS):
            mid[here, quarter * QUARTER : (quarter + 1) * QUARTER] = (
                resid[half, quarter].astype(F32) * scale
            ).astype(BF16)

    def exchange(half, outward, source, middle, final, first_sem, second_sem):
        at = other if outward else mirror
        source, middle, final = source.at[half], middle.at[half], final.at[half]

        def copy(src, dst, sem, index, offset):
            return pltpu.make_async_remote_copy(
                src_ref=src,
                dst_ref=dst,
                send_sem=sem.at[half, 0, index],
                recv_sem=sem.at[half, 1, index],
                device_id={"dev": at(offset)},
                device_id_type=MESH,
            )

        def along_x(dx):
            return copy(source.at[dx, 0], middle.at[dx, 0], first_sem, dx, 8 * dx)

        def along_z(dz):
            return copy(source.at[:, 1, dz], middle.at[:, 1, dz], first_sem, 4 + dz, 4 + dz)

        def then_z(dx, dz):
            origin = source if dx == 0 else middle
            return copy(origin.at[dx, 0, dz], final.at[dx, 0, dz], second_sem, 8 * dx + dz, dz)

        def then_x(dx, dz):
            origin, place = middle.at[dx, 1, dz], final.at[dx, 1, dz]
            return copy(origin, place, second_sem, 8 * dx + 4 + dz, 8 * dx)

        def start():
            for dx, dz in ((2, 2), (1, 1), (3, 3)):
                along_x(dx).start()
                along_z(dz).start()
            along_z(0).start()

        def forward():
            along_z(0).wait()
            for dx in (2, 1, 3):
                then_x(dx, 0).start()
            for dx, dz in ((1, 1), (3, 3), (2, 2)):
                if dx == 2:
                    for near in (2, 1, 3):
                        then_z(0, near).start()
                along_x(dx).wait()
                for far in (2, 1, 3):
                    then_z(dx, far).start()
                along_z(dz).wait()
                for far in (2, 1, 3):
                    then_x(far, dz).start()
            final[0, 0, 0] = source[0, 0, 0]
            for place in range(1, 4):
                final[place, 0, 0] = middle[place, 0, 0]
            for place in range(4):
                final[0, 1, place] = middle[0, 1, place]

        def finish():
            for dx in range(4):
                for dz in range(4):
                    if dz:
                        then_z(dx, dz).wait()
                    if dx:
                        then_x(dx, dz).wait()

        return start, forward, finish

    going = []
    for half in range(2):
        pieces = [
            mid[:, quarter * QUARTER + 256 * half : quarter * QUARTER + 256 * half + 256]
            for quarter in range(N_GROUPS)
        ]
        wide = [jnp.concatenate(pieces[2 * k : 2 * k + 2], axis=1) for k in range(2)]
        packed = dot(sel_a[...], jnp.concatenate(wide, axis=0)).astype(BF16)
        send[half, :, :, :, :, :512] = packed.reshape(4, 2, 4, 16, 512)
        narrow = [pieces[k // 2][:, 128 * (k % 2) : 128 * (k % 2) + 128] for k in range(8)]
        packed = dot(sel_b[...], jnp.concatenate(narrow, axis=0)).astype(BF16)
        send[half, :, :, :, :, 512:] = packed.reshape(4, 2, 4, 16, 128)
        going.append(
            exchange(half, True, send, relay, recv, go_first, go_second)
        )
        going[half][0]()
    going[0][1]()
    going[1][1]()

    row, col = iota((ROWS, ROWS), 0), iota((ROWS, ROWS), 1)
    unpack = one_hot(((row % 64) // 2) * 16 + (row // 64) * 2 + row % 2 == col)
    pack = one_hot(((col % 64) // 2) * 16 + (col // 64) * 2 + col % 2 == row)

    for load in load_gate_up:
        load.wait()
    load_down.wait()

    for half in range(2):
        going[half][2]()
        got = recv[half, :, :, :, :, :512].reshape(N_MEMBERS, 16, 512).astype(F32)
        last = recv[half, :, :, :, :, 512:].reshape(ROWS, 128)
        last = dot(unpack, last).astype(BF16)
        for quarter in range(N_GROUPS):
            k, place = quarter // 2, 256 * (quarter % 2)
            start = 256 * quarter
            rows[:256, start : start + 256] = (
                got[:, 8 * k : 8 * k + 8, place : place + 256].reshape(256, 256).astype(BF16)
            )
            for j in range(2):
                at = 64 * (2 * quarter + j)
                rows[256:, start + 128 * j : start + 128 * j + 128] = last[at : at + 64]
        for chunk in range(6):
            columns = slice(256 * chunk, 256 * chunk + 256)
            product = dot(rows[...], gate_up[half, :, columns])
            if half == 0:
                inner_sums[:, columns] = product
            else:
                inner_sums[:, columns] += product
    gate = inner_sums[:, :FF]
    acts[...] = (gate / (1.0 + jnp.exp(-gate)) * inner_sums[:, FF:]).astype(BF16)
    coming = []
    for half in range(2):
        for quarter in range(N_GROUPS):
            k, place = quarter // 2, 256 * (quarter % 2)
            start = quarter * QUARTER + 256 * half
            result = dot(acts[...], down[:, start : start + 256])
            back[half, :, :, :, 8 * k : 8 * k + 8, place : place + 256] = (
                result[:256].astype(BF16).reshape(4, 2, 4, 8, 256)
            )
            for j in range(2):
                at = 64 * (2 * quarter + j)
                made[at : at + 64] = result[256:, 128 * j : 128 * j + 128].astype(BF16)
        back[half, :, :, :, :, 512:] = (
            dot(pack, made[...]).astype(BF16).reshape(4, 2, 4, 16, 128)
        )
        coming.append(
            exchange(half, False, back, back_relay, home, back_first, back_second)
        )
        coming[half][0]()
    gather = one_hot(
        other(iota((EXPERTS, ROWS), 1) // 16) + base == iota((EXPERTS, ROWS), 0)
    )
    row, col = iota((2 * TOKENS, ROWS), 0), iota((2 * TOKENS, ROWS), 1)
    mask_a = (dot(code_a, gather) == (col % 8).astype(F32)) & ((col // 8) % 2 == row // TOKENS)
    row, col = iota((8 * TOKENS, ROWS), 0), iota((8 * TOKENS, ROWS), 1)
    mask_b = (dot(code_b, gather) == (8 + col % 2).astype(F32)) & ((col // 2) % 8 == row // TOKENS)

    small_loads[3].wait()
    logits = dot(mid[...], router_ref[...])
    top = jnp.max(jnp.where(hit, logits, -jnp.inf), axis=-1, keepdims=True)
    raised = jnp.where(hit, jnp.exp(logits - top), 0.0)
    gates = raised / jnp.sum(raised, axis=-1, keepdims=True)
    rest = gates
    for term in range(3):
        piece = rest.astype(BF16)
        rest = rest - piece.astype(F32)
        spread_a = dot(jnp.concatenate([piece] * 2, axis=0), gather)
        comb = jnp.where(mask_a, spread_a, 0.0).astype(BF16)
        for k in range(2):
            comb_a[k, term * TOKENS : (term + 1) * TOKENS] = comb[k * TOKENS : (k + 1) * TOKENS]
        spread_b = dot(jnp.concatenate([piece] * 8, axis=0), gather)
        comb = jnp.where(mask_b, spread_b, 0.0).astype(BF16)
        for k in range(8):
            comb_b[k, term * TOKENS : (term + 1) * TOKENS] = comb[k * TOKENS : (k + 1) * TOKENS]
    coming[0][1]()
    coming[1][1]()

    def moe_copy(half, offset):
        return pltpu.make_async_remote_copy(
            src_ref=moe_out.at[half, offset],
            dst_ref=moe_in.at[half, offset],
            send_sem=fin_sem.at[0, half, offset],
            recv_sem=fin_sem.at[1, half, offset],
            device_id={"ga": peer(offset)},
            device_id_type=MESH,
        )

    for half in range(2):
        coming[half][2]()
        for offset in order:
            quarter = peer(offset)
            place = pl.ds(pl.multiple_of((quarter % 2) * 256, 256), 256)
            wide = home[half, :, :, :, :, place].reshape(ROWS, 256)
            summed = dot(comb_a[quarter // 2], wide)
            last = home[half, :, :, :, :, 512:].reshape(ROWS, 128)
            more = [dot(comb_b[2 * quarter + j], last) for j in range(2)]
            summed = summed + jnp.concatenate(more, axis=1)
            moe_out[half, offset] = (
                summed[:TOKENS] + summed[TOKENS : 2 * TOKENS] + summed[2 * TOKENS :]
            )
            if offset:
                moe_copy(half, offset).start()
    base = jnp.concatenate([resid[0, group], resid[1, group]], axis=0).astype(F32)
    for half in range(2):
        columns = slice(256 * half, 256 * half + 256)
        for offset in (1, 3, 2):
            moe_copy(half, offset).wait()
        moe = moe_out[half, 0] + moe_in[half, 1] + moe_in[half, 2] + moe_in[half, 3]
        final = base[:, columns] + moe
        out_ref[:, :, columns] = final.reshape(REQUESTS, 2, 256).astype(BF16)


def layer(lengths, hidden, w_router, routes, w_qkv, cache, w_out, gate_up, down):
    vmem = pl.BlockSpec(memory_space=pltpu.VMEM)
    hbm = pl.BlockSpec(memory_space=pl.ANY)
    dma = pltpu.SemaphoreType.DMA
    packed = pltpu.VMEM((2, 4, 2, 4, 16, PACKED), BF16)
    parts = pltpu.VMEM((2, N_GROUPS, 32, QUARTER), F32)
    sums = pltpu.VMEM((2, N_GROUPS, TOKENS, 256), F32)
    return pl.pallas_call(
        layer_kernel,
        out_shape=jax.ShapeDtypeStruct((REQUESTS, 2, QUARTER), BF16),
        in_specs=[hbm] * 9,
        out_specs=vmem,
        scratch_shapes=[
            pltpu.SMEM((REQUESTS,), jnp.int32),
            pltpu.VMEM((REQUESTS, 2, WIDTH), BF16),
            pltpu.VMEM((WIDTH, EXPERTS), BF16),
            pltpu.VMEM((2, 8, REQUESTS), jnp.int32),
            pltpu.VMEM((5, WIDTH, 256), BF16),
            pltpu.VMEM((REQUESTS, 2, CONTEXT, HD), BF16),
            pltpu.VMEM((TOKENS, WIDTH), BF16),
            pltpu.VMEM((ROWS, HD), BF16),
            pltpu.VMEM((N_GROUPS, 1024, QUARTER), BF16),
            pltpu.VMEM((2, WIDTH // 2, 2 * FF), BF16),
            pltpu.VMEM((FF, WIDTH), BF16),
            parts,
            parts,
            pltpu.VMEM((2, N_GROUPS, 32, QUARTER), BF16),
            pltpu.VMEM((TOKENS, WIDTH), BF16),
            pltpu.VMEM((ROWS, 2 * TOKENS), BF16),
            pltpu.VMEM((ROWS, 8 * TOKENS), BF16),
            pltpu.VMEM((2, 3 * TOKENS, ROWS), BF16),
            pltpu.VMEM((8, 3 * TOKENS, ROWS), BF16),
            packed,
            packed,
            packed,
            packed,
            packed,
            packed,
            pltpu.VMEM((320, WIDTH // 2), BF16),
            pltpu.VMEM((320, 2 * FF), F32),
            pltpu.VMEM((320, FF), BF16),
            pltpu.VMEM((ROWS, 128), BF16),
            sums,
            sums,
            dma((4,)),
            dma((5,)),
            dma((REQUESTS // BATCH,)),
            dma((5,)),
            dma((2, N_GROUPS)),
            dma((2, 2, N_GROUPS)),
            dma((2, 2, N_GROUPS)),
            dma((2, 2, 8)),
            dma((2, 2, N_MEMBERS)),
            dma((2, 2, 8)),
            dma((2, 2, N_MEMBERS)),
            dma((2, 2, N_GROUPS)),
        ],
        compiler_params=pltpu.CompilerParams(
            collective_id=0, has_side_effects=True, vmem_limit_bytes=56 * 1024 * 1024
        ),
    )(lengths, hidden, w_router, routes, w_qkv, cache, w_out, gate_up, down)


def body(hidden_in, w_qkv, w_out, cache, lengths, w_router, routes, w_gate_up, w_down):
    return layer(
        lengths,
        hidden_in,
        w_router,
        jnp.transpose(routes, (1, 2, 0)),
        w_qkv[:, 0],
        cache[:, 0],
        w_out[0],
        w_gate_up[0],
        w_down[0],
    )


def solution(mesh):
    return jax.shard_map(
        body,
        mesh=mesh,
        in_specs=(
            P("dev", None, None),
            P(None, "ga", None),
            P("ga", None, None),
            P("dev", "ga", None, None, None),
            P("dev"),
            P(),
            P("dev", None, None),
            P(("ga", "dev"), None, None),
            P(("ga", "dev"), None, None),
        ),
        out_specs=P("dev", None, "ga"),
        check_vma=False,
    )
```
